32 devices in a mesh: sec: 4 (over y, core), tile: 8 (over z, x).
Axes of the slice: x: 2, y: 2, z: 4, core: 2. Of those that a mesh axis runs over, the one named last changes fastest.
Arguments:
- tile_strips: bfloat16 [4, 8, 2, 5, 64, 512], P('sec', 'tile'), may hold values from -6 to 6, as said below
- pair_mask: int32 [4, 8, 2, 3], P('sec', 'tile'), may hold values 0 or 1
- strip_offset: int32 [4, 8, 2, 3, 2], P('sec', 'tile'), may hold values from -16 to 16
- stiffness: float32 [4, 8, 2], P('sec', 'tile'), may hold values from 0.05 to 0.5
Outputs:
- affine_update: float32 [6, 4, 8, 2], P(None, 'sec', 'tile')
- residual: float32 [6, 4, 8, 2], P(None, 'sec', 'tile')
The draws below stay inside these ranges and needn't reach their ends.
Inputs may be any that keep to these rules, and one draw needn't show every extreme that they name: `tile_strips`: neighbouring tiles' intersecting images are correlated.
All inputs are finite; a program needn't handle non-finite values. No bound on the sum of `pair_mask` on one device may be relied on, other than what follows from the above.
Results may differ from the reference program's by a relative error of at most 0.0013.
Values may be sent and summed in bfloat16 or wider, within the bound.
A program may use at most 64 MiB of HBM per device.

```python
import math
import jax
import jax.numpy as jnp
from jax import lax

GRID_C = 2
STRIP_H = 64
STRIP_W = 512
ITERS = 3
SECTIONS = 4
GRID_R = 8


def draw_tile_strips(key, part):
    keys = jax.random.split(key, 7)
    full = (SECTIONS, GRID_R, GRID_C, STRIP_H, STRIP_W)
    own_right = jax.random.normal(keys[0], full, jnp.float32)
    own_bottom = jax.random.normal(keys[1], full, jnp.float32)
    patches = jax.random.normal(keys[2], full, jnp.float32)
    first_left = jax.random.normal(keys[3], (SECTIONS, GRID_R, 1, STRIP_H, STRIP_W), jnp.float32)
    fresh_left = jax.random.normal(keys[4], (SECTIONS, GRID_R, GRID_C - 1, STRIP_H, STRIP_W), jnp.float32)
    first_top = jax.random.normal(keys[5], (SECTIONS, 1, GRID_C, STRIP_H, STRIP_W), jnp.float32)
    fresh_top = jax.random.normal(keys[6], (SECTIONS, GRID_R - 1, GRID_C, STRIP_H, STRIP_W), jnp.float32)
    left = jnp.concatenate([first_left, 0.8 * jnp.roll(own_right, 1, axis=4)[:, :, :-1] + 0.6 * fresh_left], axis=2)
    top = jnp.concatenate([first_top, 0.8 * jnp.roll(own_bottom, 1, axis=3)[:, :-1] + 0.6 * fresh_top], axis=1)
    chain = [patches[0]]
    for index in range(1, SECTIONS):
        chain.append(0.8 * jnp.roll(chain[-1], 1, axis=3) + 0.6 * patches[index])
    patch = jnp.stack(chain)
    strips = jnp.stack([left, own_right, top, own_bottom, patch], axis=3)
    return jnp.clip(strips, -6.0, 6.0).astype(jnp.bfloat16)


def place_ends(entries, own_key, least, top_value):
    longest = entries.shape.index(max(entries.shape))
    spots = []
    for shift in (0, 1):
        where = [jax.random.randint(jax.random.fold_in(own_key, axis), (), 0, length) for axis, length in enumerate(entries.shape)]
        where[longest] = (where[longest] + shift) % entries.shape[longest]
        spots.append(tuple(where))
    return entries.at[spots[0]].set(least).at[spots[1]].set(top_value)


def steps_of(rng, extent, shards, smallest, high):
    level = 1.0
    for position, blocks in shards:
        heights = jax.random.uniform(jax.random.fold_in(jax.random.fold_in(rng, 6), position), (blocks,), jnp.float32, smallest / len(shards), high / len(shards))
        level = level * jnp.repeat(jnp.exp(heights), extent[position] // blocks).reshape((-1,) + (1,) * (len(extent) - 1 - position))
    return level


def setup_inputs(seed: int = 0) -> dict:
    key_list = jax.random.split(jax.random.key(seed), 5)
    return {
        "tile_strips": draw_tile_strips(jax.random.fold_in(key_list[4], 71), 0),
        "pair_mask": place_ends((jax.random.randint(key_list[1], (SECTIONS, GRID_R, GRID_C, 3), 0, 5) < 4).astype(jnp.int32), jax.random.fold_in(key_list[1], 1), 0, 1),
        "strip_offset": place_ends(jax.random.randint(key_list[2], (SECTIONS, GRID_R, GRID_C, 3, 2), -(STRIP_H // 4), STRIP_H // 4 + 1), jax.random.fold_in(key_list[2], 1), -(STRIP_H // 4), (STRIP_H // 4 + 1) - 1).astype(jnp.int32),
        "stiffness": jnp.clip(jnp.exp(math.log(0.5) - 2.3025851 * jax.random.uniform(key_list[3], (SECTIONS, GRID_R, GRID_C), jnp.float32) ** steps_of(key_list[3], (SECTIONS, GRID_R, GRID_C), ((0, 4), (1, 8)), -0.2, 0.2)), 0.05, 0.5),
    }


highest = lax.Precision.HIGHEST

def strip_gradients(image):
    padded = jnp.pad(image, 1)
    along_x = (padded[1:-1, 2:] - padded[1:-1, :-2]) * 0.5
    along_y = (padded[2:, 1:-1] - padded[:-2, 1:-1]) * 0.5
    return (along_x, along_y)

def jacobian_rows(image, shift_x, shift_y):
    height, width = image.shape
    column_grid = jnp.arange(width, dtype=jnp.float32)[None, :]
    row_grid = jnp.arange(height, dtype=jnp.float32)[:, None]
    coord_u = (column_grid + shift_x) / width - 0.5
    coord_v = (row_grid + shift_y) / height - 0.5
    along_x, along_y = strip_gradients(image)
    stacked = jnp.stack([along_x * coord_u, along_x * coord_v, along_x, along_y * coord_u, along_y * coord_v, along_y])
    return stacked.reshape(6, height * width)

def pair_block(image_a, image_b, offset):
    first = image_a.astype(jnp.float32)
    second = image_b.astype(jnp.float32)
    shifts = offset.astype(jnp.float32)
    zero = jnp.zeros((), jnp.float32)
    jacobian = jnp.concatenate([jacobian_rows(first, zero, zero), -jacobian_rows(second, shifts[0], shifts[1])], axis=0)
    pixels = first.shape[0] * first.shape[1]
    misfit = (first - second).reshape(pixels)
    normal = jnp.dot(jacobian, jacobian.T, precision=highest, preferred_element_type=jnp.float32) / pixels
    pull = -jnp.dot(jacobian, misfit, precision=highest, preferred_element_type=jnp.float32) / pixels
    return (normal, pull)

def to_next(array, axis):
    lead = jnp.zeros_like(lax.slice_in_dim(array, 0, 1, axis=axis))
    return jnp.concatenate([lead, lax.slice_in_dim(array, 0, array.shape[axis] - 1, axis=axis)], axis=axis)

def from_next(array, axis):
    tail = jnp.zeros_like(lax.slice_in_dim(array, 0, 1, axis=axis))
    return jnp.concatenate([lax.slice_in_dim(array, 1, array.shape[axis], axis=axis), tail], axis=axis)

def apply_block(block, vector):
    return jnp.einsum('ij...,j...->i...', block, vector, precision=highest)

def cholesky_rows(matrix):
    order = matrix.shape[0]
    factor = [[None] * order for index in range(order)]
    for column in range(order):
        pivot = matrix[column, column]
        for inner in range(column):
            pivot = pivot - factor[column][inner] * factor[column][inner]
        pivot = jnp.sqrt(pivot)
        factor[column][column] = pivot
        for row in range(column + 1, order):
            entry = matrix[row, column]
            for inner in range(column):
                entry = entry - factor[row][inner] * factor[column][inner]
            factor[row][column] = entry / pivot
    return factor

def solve_rows(factor, vector):
    order = len(factor)
    forward = []
    for row in range(order):
        value = vector[row]
        for inner in range(row):
            value = value - factor[row][inner] * forward[inner]
        forward.append(value / factor[row][row])
    backward = [None] * order
    for row in reversed(range(order)):
        value = forward[row]
        for inner in range(row + 1, order):
            value = value - factor[inner][row] * backward[inner]
        backward[row] = value / factor[row][row]
    return jnp.stack(backward)

def grid_blocks(images_a, images_b, offsets, exists):
    sections, tile_rows, columns, height, width = images_a.shape
    flat = (images_a.reshape(sections * tile_rows, columns, height, width), images_b.reshape(sections * tile_rows, columns, height, width), offsets.reshape(sections * tile_rows, columns, 2))
    normal, pull = lax.map(lambda items: jax.vmap(pair_block)(items[0], items[1], items[2]), flat)
    normal = normal.reshape(sections, tile_rows, columns, 12, 12).transpose(3, 4, 0, 1, 2) * exists
    pull = pull.reshape(sections, tile_rows, columns, 12).transpose(3, 0, 1, 2) * exists
    return (normal, pull)

def reference(tile_strips, pair_mask, strip_offset, stiffness):
    sections, tile_rows, columns = (tile_strips.shape[0], tile_strips.shape[1], tile_strips.shape[2])
    section_index = jnp.arange(sections)[:, None, None]
    row_index = jnp.arange(tile_rows)[None, :, None]
    column_index = jnp.arange(columns)[None, None, :]
    exists_right = ((pair_mask[..., 0] == 1) & (column_index < columns - 1)).astype(jnp.float32)
    exists_down = ((pair_mask[..., 1] == 1) & (row_index < tile_rows - 1)).astype(jnp.float32)
    exists_cross = ((pair_mask[..., 2] == 1) & (section_index < sections - 1)).astype(jnp.float32)
    normal_right, pull_right = grid_blocks(tile_strips[:, :, :, 1], from_next(tile_strips[:, :, :, 0], 2), strip_offset[:, :, :, 0], exists_right)
    normal_down, pull_down = grid_blocks(tile_strips[:, :, :, 3], from_next(tile_strips[:, :, :, 2], 1), strip_offset[:, :, :, 1], exists_down)
    normal_cross, pull_cross = grid_blocks(tile_strips[:, :, :, 4], from_next(tile_strips[:, :, :, 4], 0), strip_offset[:, :, :, 2], exists_cross)
    identity = jnp.eye(6, dtype=jnp.float32)[:, :, None, None, None]
    diagonal = stiffness[None, None] * identity + normal_right[:6, :6] + to_next(normal_right[6:, 6:], 4)
    diagonal = diagonal + normal_down[:6, :6] + to_next(normal_down[6:, 6:], 3)
    diagonal = diagonal + normal_cross[:6, :6] + to_next(normal_cross[6:, 6:], 2)
    load = pull_right[:6] + to_next(pull_right[6:], 3) + pull_down[:6] + to_next(pull_down[6:], 2)
    load = load + pull_cross[:6] + to_next(pull_cross[6:], 1)
    couplings = ((normal_right[:6, 6:], 3), (normal_down[:6, 6:], 2), (normal_cross[:6, 6:], 1))

    def multiply(vector):
        result = apply_block(diagonal, vector)
        for coupling, axis in couplings:
            result = result + apply_block(coupling, from_next(vector, axis))
            result = result + to_next(apply_block(jnp.swapaxes(coupling, 0, 1), vector), axis)
        return result
    factor = cholesky_rows(diagonal)
    affine_update = jnp.zeros_like(load)
    residual = load
    scaled = solve_rows(factor, residual)
    direction = scaled
    rho_now = jnp.sum(residual * scaled)
    for step in range(ITERS):
        product = multiply(direction)
        step_size = rho_now / jnp.sum(direction * product)
        affine_update = affine_update + step_size * direction
        residual = residual - step_size * product
        scaled = solve_rows(factor, residual)
        rho_next = jnp.sum(residual * scaled)
        direction = scaled + rho_next / rho_now * direction
        rho_now = rho_next
    return (affine_update, residual)
```

```python
import functools

import jax
import jax.numpy as jnp
from jax import lax
from jax.experimental import pallas as pl
from jax.experimental.pallas import tpu as pltpu
from jax.sharding import PartitionSpec as P

ITERS = 3
LANES = 128
SUB = 8
IMAGES = 5
KINDS = 3
BLOCK = 6 * SUB
QROWS = 4
MESH = pl.DeviceIdType.MESH

PLACES = (
    ((2, 2),),
    ((0, 2), (2, 0)),
    ((1, 2), (2, 1)),
    ((0, 0),),
    ((0, 1), (1, 0)),
    ((1, 1),),
)
SELF_AT = tuple((image // 2, BLOCK * (image % 2)) for image in range(IMAGES))
PAIR_AT = ((2, BLOCK), (3, 0), (3, BLOCK))
PULL_AT = ((2, 96), (3, 96), (3, 112))
OFFSET_AT = (0, 96)
STIFF_AT = (0, 120)
EXISTS_AT = (1, 96)
ENDS = ((1, 0), (3, 2), (4, 4))


def round_up(value, unit):
    return (value + unit - 1) // unit * unit


def column_moments(fields, width, quadratic):
    groups = fields.groups
    sums = None
    for k in range(groups):
        values = fields(k)
        if sums is None:
            sums = [[value] * (3 if quadratic else 2) for value in values]
        else:
            for entry, value in zip(sums, values):
                entry[0] = entry[0] + value
                entry[1] = entry[1] + entry[0]
                if quadratic:
                    entry[2] = entry[2] + entry[1]
    height = groups * SUB
    step = SUB / height
    row = lax.broadcasted_iota(jnp.int32, (SUB, width), 0).astype(jnp.float32)
    column = lax.broadcasted_iota(jnp.int32, (SUB, width), 1).astype(jnp.float32)
    edge = row / height + 0.5
    u = column / width - 0.5

    def fold(array):
        total = array[:, :LANES]
        for start in range(LANES, width, LANES):
            total = total + array[:, start : start + LANES]
        return jnp.sum(total, axis=0, keepdims=True)

    out = []
    for entry in sums:
        zeroth = entry[0]
        first = edge * zeroth - step * entry[1]
        scaled = u * zeroth
        moments = [fold(zeroth), fold(scaled), fold(first)]
        if quadratic:
            second = (
                edge * edge * zeroth
                - (2.0 * step) * edge * entry[1]
                + (step * step) * (2.0 * entry[2] - entry[1])
            )
            moments += [fold(u * scaled), fold(u * first), fold(second)]
        out.append(moments)
    return out


class Products:
    def __init__(self, groups, form):
        self.groups = groups
        self.form = form

    def __call__(self, k):
        return self.form(k)


def apply_columns(columns, vector):
    total = columns[0] * vector[0:1]
    for j in range(1, 6):
        total = total + columns[j] * vector[j : j + 1]
    return total


def inverse_columns(columns, sublane):
    columns = list(columns)
    for p in range(6):
        pivot = 1.0 / columns[p][p : p + 1]
        here = sublane == p
        lead = columns[p]
        for j in range(6):
            if j != p:
                ratio = columns[j][p : p + 1] * pivot
                columns[j] = jnp.where(here, ratio, columns[j] - lead * ratio)
        columns[p] = jnp.where(here, pivot, -lead * pivot)
    return columns


def transposed_columns(columns, sublane):
    out = []
    for i in range(6):
        total = jnp.zeros_like(columns[0])
        for j in range(6):
            total = jnp.where(sublane == j, columns[j][i : i + 1], total)
        out.append(total)
    return out


def kernel(
    sections,
    tile_rows,
    strips_hbm,
    mask_ref,
    offset_ref,
    stiff_ref,
    update_ref,
    residual_ref,
    strips,
    landed,
    grad_x,
    grad_y,
    rows,
    gathered,
    local_sem,
    strip_send,
    strip_recv,
    gather_send,
    gather_recv,
):
    columns, _, height, width = strips.shape
    count = sections * tile_rows
    per_device = gathered.shape[0] // count
    groups = height // SUB
    own_images = columns * IMAGES
    section = lax.axis_index("sec")
    tile_row = lax.axis_index("tile")
    me = section * tile_rows + tile_row

    def device(step):
        other = lax.rem(me + step, count)
        return (other // tile_rows, lax.rem(other, tile_rows))

    barrier = pltpu.get_barrier_semaphore()

    @pl.loop(1, count)
    def _(step):
        pl.semaphore_signal(barrier, inc=1, device_id=device(step), device_id_type=MESH)

    local = pltpu.make_async_copy(strips_hbm, strips, local_sem)
    local.start()

    def band(size, sign):
        first = lax.broadcasted_iota(jnp.int32, (size, size), 0)
        second = lax.broadcasted_iota(jnp.int32, (size, size), 1)
        gap = (first - second) * sign
        return jnp.where(gap == 1, 0.5, jnp.where(gap == -1, -0.5, 0.0)).astype(jnp.bfloat16)

    along = band(width, 1)
    down = band(height, -1)
    rows[...] = jnp.zeros_like(rows)

    pl.semaphore_wait(barrier, count - 1)

    def strip_copy(kind, c):
        target = (section, tile_row - 1) if kind == 0 else (section - 1, tile_row)
        return pltpu.make_async_remote_copy(
            src_ref=strips_hbm.at[c, 2 if kind == 0 else 4],
            dst_ref=landed.at[kind, c],
            send_sem=strip_send.at[kind, c],
            recv_sem=strip_recv.at[kind, c],
            device_id=target,
            device_id_type=MESH,
        )

    sends = (tile_row > 0, section > 0)
    receives = (tile_row < tile_rows - 1, section < sections - 1)
    for kind in range(2):

        @pl.when(sends[kind])
        def _():
            for c in range(columns):
                strip_copy(kind, c).start()

    local.wait()

    def gradients(images, start):
        total = images.shape[0] * height
        grad_x[pl.ds(start * height, total), :] = jnp.dot(
            images.reshape(total, width), along, preferred_element_type=jnp.float32
        )
        for index in range(images.shape[0]):
            grad_y[pl.ds((start + index) * height, height), :] = jnp.dot(
                down, images[index], preferred_element_type=jnp.float32
            )

    gradients(strips[...].reshape(own_images, height, width), 0)

    def group(ref, image, k):
        return ref[pl.ds(pl.multiple_of(image * height + k * SUB, SUB), SUB), :]

    def put(row, value):
        rows[pl.ds(row, 1), :] = value

    def self_blocks(c, image, spot):
        at = c * IMAGES + image

        def form(k):
            x, y = group(grad_x, at, k), group(grad_y, at, k)
            return (x * x, x * y, y * y)

        moments = column_moments(Products(groups, form), width, True)
        base = (c * QROWS + spot[0]) * LANES + spot[1]
        for p, q, entry in ((0, 0, moments[0]), (0, 1, moments[1]), (1, 1, moments[2])):
            for places, value in zip(PLACES, entry):
                for a, b in places:
                    put(base + SUB * (3 * q + b) + 3 * p + a, value)
                    if p != q:
                        put(base + SUB * (3 * p + b) + 3 * q + a, value)

    def pair_blocks(kind, c, at_a, at_b, image_a, image_b):
        def cross(k):
            xa, ya = group(grad_x, at_a, k), group(grad_y, at_a, k)
            xb, yb = group(grad_x, at_b, k), group(grad_y, at_b, k)
            return (xa * xb, xa * yb, ya * xb, ya * yb)

        misfit = image_a.astype(jnp.float32) - image_b.astype(jnp.float32)

        def pulls(k):
            miss = misfit[k * SUB : (k + 1) * SUB]
            return (
                group(grad_x, at_a, k) * miss,
                group(grad_y, at_a, k) * miss,
                group(grad_x, at_b, k) * miss,
                group(grad_y, at_b, k) * miss,
            )

        base = (c * QROWS + PAIR_AT[kind][0]) * LANES + PAIR_AT[kind][1]
        for index, entry in enumerate(column_moments(Products(groups, cross), width, True)):
            p, q = divmod(index, 2)
            for places, value in zip(PLACES, entry):
                for a, b in places:
                    put(base + SUB * (3 * q + b) + 3 * p + a, -value)
        base = (c * QROWS + PULL_AT[kind][0]) * LANES + PULL_AT[kind][1]
        for index, entry in enumerate(column_moments(Products(groups, pulls), width, False)):
            side, p = divmod(index, 2)
            for weight, value in zip((2, 0, 1), entry):
                put(base + SUB * side + 3 * p + weight, value if side else -value)

    for image in range(IMAGES):

        @pl.loop(0, columns)
        def _(c):
            self_blocks(c, image, SELF_AT[image])

    @pl.loop(0, columns - 1)
    def _(c):
        pair_blocks(
            0, c, c * IMAGES + 1, (c + 1) * IMAGES, strips[c, 1], strips[c + 1, 0]
        )

    for kind in range(2):

        @pl.when(receives[kind])
        def _():
            for c in range(columns):
                strip_copy(kind, c).wait_recv()
            gradients(landed[kind], own_images + kind * columns)

            @pl.loop(0, columns)
            def _(c):
                image = ENDS[kind + 1][0]
                pair_blocks(
                    kind + 1,
                    c,
                    c * IMAGES + image,
                    own_images + kind * columns + c,
                    strips[c, image],
                    landed[kind, c],
                )

    ones = jnp.ones((SUB, LANES), jnp.bfloat16)
    lane = lax.broadcasted_iota(jnp.int32, (1, LANES), 1)
    contract = (((1,), (1,)), ((), ()))
    mine = pl.multiple_of(me * per_device, SUB)

    def exists(c, kind):
        inside = (jnp.int32(c) < columns - 1, receives[0], receives[1])[kind]
        return jnp.where((mask_ref[c, kind] == 1) & inside, 1.0, 0.0)

    for c in range(columns):
        for h in range(QROWS):
            part = rows[(c * QROWS + h) * LANES : (c * QROWS + h + 1) * LANES, :]
            high = part.astype(jnp.bfloat16)
            low = (part - high.astype(jnp.float32)).astype(jnp.bfloat16)
            summed = lax.dot_general(ones, high, contract, preferred_element_type=jnp.float32)
            summed = summed + lax.dot_general(ones, low, contract, preferred_element_type=jnp.float32)
            line = summed[0:1] * (1.0 / (height * width))
            if h == 0:
                for kind in range(KINDS):
                    start = OFFSET_AT[1] + SUB * kind
                    for axis, extent in ((0, width), (1, height)):
                        shift = offset_ref[c, kind, axis].astype(jnp.float32) / extent
                        here = (lane == start + axis) | (lane == start + 3 + axis)
                        line = jnp.where(here, shift, line)
                line = jnp.where(lane >= STIFF_AT[1], stiff_ref[c], line)
            if h == 1:
                for kind in range(KINDS):
                    start = EXISTS_AT[1] + SUB * kind
                    here = (lane >= start) & (lane < start + SUB)
                    line = jnp.where(here, exists(c, kind), line)
            gathered[pl.ds(mine + c * QROWS + h, 1), :] = line

    @pl.loop(1, count)
    def _(step):
        pltpu.make_async_remote_copy(
            src_ref=gathered.at[pl.ds(mine, per_device)],
            dst_ref=gathered.at[pl.ds(mine, per_device)],
            send_sem=gather_send,
            recv_sem=gather_recv,
            device_id=device(step),
            device_id_type=MESH,
        ).start()

    others = gathered.at[pl.ds(0, (count - 1) * per_device)]
    pltpu.make_async_copy(others, others, gather_recv).wait()

    tiles = columns * count
    padded = round_up(tiles, LANES)
    tables = []
    for h in range(QROWS):
        parts = [
            gathered[pl.ds(c * QROWS + h, count, stride=per_device), :] for c in range(columns)
        ]
        if padded > tiles:
            parts.append(jnp.zeros((padded - tiles, LANES), jnp.float32))
        tables.append(jnp.concatenate(parts, axis=0).T)

    def vector_at(spot, index=0):
        start = spot[1] + SUB * index
        return tables[spot[0]][start : start + SUB]

    def columns_at(spot):
        return [vector_at(spot, j) for j in range(6)]

    sublane = lax.broadcasted_iota(jnp.int32, (SUB, padded), 0)
    place = lax.broadcasted_iota(jnp.int32, (SUB, padded), 1)

    def to_next(array, by):
        return pltpu.roll(array, by, 1)

    def from_next(array, by):
        return pltpu.roll(array, padded - by, 1)

    shifts = (count, 1, tile_rows)
    stiffness = jnp.where(place < tiles, vector_at(STIFF_AT), 1.0)
    diagonal = [jnp.where(sublane == j, stiffness, 0.0) for j in range(6)]
    load = jnp.zeros((SUB, padded), jnp.float32)
    couplings = []
    for kind in range(KINDS):
        by = shifts[kind]
        there = vector_at(EXISTS_AT, kind)
        offset = vector_at(OFFSET_AT, kind)
        du, dv = offset[0:1], offset[1:2]

        def shift_rows(vector):
            return vector + offset * jnp.where(sublane < 3, vector[2:3], vector[5:6])

        def shift_columns(block):
            out = []
            for p in range(2):
                last = block[3 * p + 2]
                out += [block[3 * p] + du * last, block[3 * p + 1] + dv * last, last]
            return out

        block_a = columns_at(SELF_AT[ENDS[kind][0]])
        block_b = [from_next(column, by) for column in columns_at(SELF_AT[ENDS[kind][1]])]
        block_b = [shift_rows(column) for column in shift_columns(block_b)]
        for j in range(6):
            diagonal[j] = diagonal[j] + there * block_a[j] + to_next(there * block_b[j], by)
        pull_a = vector_at(PULL_AT[kind], 0)
        pull_b = shift_rows(vector_at(PULL_AT[kind], 1))
        load = load + there * pull_a + to_next(there * pull_b, by)
        coupling = [there * column for column in shift_columns(columns_at(PAIR_AT[kind]))]
        couplings.append((coupling, transposed_columns(coupling, sublane), by))

    inverse = inverse_columns(diagonal, sublane)

    def multiply(vector):
        result = apply_columns(diagonal, vector)
        for coupling, flipped, by in couplings:
            result = result + apply_columns(coupling, from_next(vector, by))
            result = result + to_next(apply_columns(flipped, vector), by)
        return result

    def total(array):
        return jnp.sum(jnp.sum(array, axis=0, keepdims=True), axis=1, keepdims=True)

    residual = load
    scaled = apply_columns(inverse, residual)
    product = multiply(scaled)
    rho_now, curve = total(residual * scaled), total(scaled * product)
    step_size = rho_now / curve
    direction, carried = scaled, product
    update = jnp.zeros_like(load)
    for step in range(ITERS):
        update = update + step_size * direction
        residual = residual - step_size * carried
        if step + 1 < ITERS:
            scaled = apply_columns(inverse, residual)
            product = multiply(scaled)
            rho_next, curve = total(residual * scaled), total(scaled * product)
            ratio = rho_next / rho_now
            step_size = rho_next / (curve - ratio * rho_next / step_size)
            direction = scaled + ratio * direction
            carried = product + ratio * carried
            rho_now = rho_next

    for out, values in ((update_ref, update), (residual_ref, residual)):
        for c in range(columns):
            own = jnp.sum(jnp.where(place == c * count + me, values, 0.0), axis=1, keepdims=True)
            out[:, c : c + 1] = own[0:6]

    pltpu.make_async_copy(others, others, gather_send).wait()
    for kind in range(2):

        @pl.when(sends[kind])
        def _():
            for c in range(columns):
                strip_copy(kind, c).wait_send()


def shards(tile_strips, pair_mask, strip_offset, stiffness):
    _, _, columns, images, height, width = tile_strips.shape
    sections = lax.axis_size("sec")
    tile_rows = lax.axis_size("tile")
    count = sections * tile_rows
    per_device = round_up(columns * QROWS, SUB)
    held = columns * (IMAGES + 2) * height
    out = jax.ShapeDtypeStruct((6, columns), jnp.float32)
    update, residual = pl.pallas_call(
        functools.partial(kernel, sections, tile_rows),
        out_shape=(out, out),
        in_specs=[
            pl.BlockSpec(memory_space=pl.ANY),
            pl.BlockSpec(memory_space=pltpu.SMEM),
            pl.BlockSpec(memory_space=pltpu.SMEM),
            pl.BlockSpec(memory_space=pltpu.SMEM),
        ],
        out_specs=(
            pl.BlockSpec(memory_space=pltpu.VMEM),
            pl.BlockSpec(memory_space=pltpu.VMEM),
        ),
        scratch_shapes=[
            pltpu.VMEM((columns, images, height, width), jnp.bfloat16),
            pltpu.VMEM((2, columns, height, width), jnp.bfloat16),
            pltpu.VMEM((held, width), jnp.float32),
            pltpu.VMEM((held, width), jnp.float32),
            pltpu.VMEM((columns * QROWS * LANES, LANES), jnp.float32),
            pltpu.VMEM((count * per_device, LANES), jnp.float32),
            pltpu.SemaphoreType.DMA,
            pltpu.SemaphoreType.DMA((2, columns)),
            pltpu.SemaphoreType.DMA((2, columns)),
            pltpu.SemaphoreType.DMA,
            pltpu.SemaphoreType.DMA,
        ],
        compiler_params=pltpu.CompilerParams(
            collective_id=0, has_side_effects=True, vmem_limit_bytes=32 * 1024 * 1024
        ),
    )(tile_strips[0, 0], pair_mask[0, 0], strip_offset[0, 0], stiffness[0, 0])
    shape = (6, 1, 1, columns)
    return update.reshape(shape), residual.reshape(shape)


def solution(mesh):
    return jax.shard_map(
        shards,
        mesh=mesh,
        in_specs=(
            P("sec", "tile", None, None, None, None),
            P("sec", "tile", None, None),
            P("sec", "tile", None, None, None),
            P("sec", "tile", None),
        ),
        out_specs=(P(None, "sec", "tile", None), P(None, "sec", "tile", None)),
        check_vma=False,
    )
```

```python
import functools

import jax
import jax.numpy as jnp
from jax import lax
from jax.experimental import pallas as pl
from jax.experimental.pallas import tpu as pltpu
from jax.sharding import PartitionSpec as P

ITERS = 3
LANES = 128
SUB = 8
IMAGES = 5
KINDS = 3
QROWS = 2
MESH = pl.DeviceIdType.MESH

QUAD = 6
MOMENT = ((3, 4, 1), (4, 5, 2), (1, 2, 0))
SELF = 3 * QUAD
CROSS = 4 * QUAD
SUM_AT = 0
SELF_AT = (SELF, 2 * SELF, 3 * SELF)
OFFSET_AT = 96
EXISTS_AT = 102
STIFF_AT = 105
PAIR_AT = (LANES, LANES + CROSS, LANES + 2 * CROSS)
PULL_A_AT = LANES + 3 * CROSS
PULL_B_AT = PULL_A_AT + 6
ENDS = ((1, 0), (3, 2), (4, 4))


def round_up(value, unit):
    return (value + unit - 1) // unit * unit


def column_moments(fields, width, quadratic):
    groups = fields.groups
    sums = None
    for k in range(groups):
        values = fields(k)
        if sums is None:
            sums = [[value] * (3 if quadratic else 2) for value in values]
        else:
            for entry, value in zip(sums, values):
                entry[0] = entry[0] + value
                entry[1] = entry[1] + entry[0]
                if quadratic:
                    entry[2] = entry[2] + entry[1]
    height = groups * SUB
    step = SUB / height
    row = lax.broadcasted_iota(jnp.int32, (SUB, width), 0).astype(jnp.float32)
    column = lax.broadcasted_iota(jnp.int32, (SUB, width), 1).astype(jnp.float32)
    edge = row / height + 0.5
    u = column / width - 0.5

    def fold(array):
        total = array[:, :LANES]
        for start in range(LANES, width, LANES):
            total = total + array[:, start : start + LANES]
        return jnp.sum(total, axis=0, keepdims=True)

    out = []
    for entry in sums:
        zeroth = entry[0]
        first = edge * zeroth - step * entry[1]
        scaled = u * zeroth
        moments = [fold(zeroth), fold(scaled), fold(first)]
        if quadratic:
            second = (
                edge * edge * zeroth
                - (2.0 * step) * edge * entry[1]
                + (step * step) * (2.0 * entry[2] - entry[1])
            )
            moments += [fold(u * scaled), fold(u * first), fold(second)]
        out.append(moments)
    return out


class Products:
    def __init__(self, groups, form):
        self.groups = groups
        self.form = form

    def __call__(self, k):
        return self.form(k)


def apply_columns(columns, vector):
    total = columns[0] * vector[0:1]
    for j in range(1, 6):
        total = total + columns[j] * vector[j : j + 1]
    return total


def inverse_columns(columns, sublane):
    columns = list(columns)
    for p in range(6):
        pivot = 1.0 / columns[p][p : p + 1]
        here = sublane == p
        lead = columns[p]
        for j in range(6):
            if j != p:
                ratio = columns[j][p : p + 1] * pivot
                columns[j] = jnp.where(here, ratio, columns[j] - lead * ratio)
        columns[p] = jnp.where(here, pivot, -lead * pivot)
    return columns


def transposed_columns(columns, sublane):
    out = []
    for i in range(6):
        total = jnp.zeros_like(columns[0])
        for j in range(6):
            total = jnp.where(sublane == j, columns[j][i : i + 1], total)
        out.append(total)
    return out


def kernel(
    sections,
    tile_rows,
    strips_hbm,
    mask_hbm,
    offset_hbm,
    stiff_hbm,
    out_ref,
    strips,
    landed,
    grad_x,
    grad_y,
    rows,
    gathered,
    table,
    mask_ref,
    offset_ref,
    stiff_ref,
    local_sem,
    strip_send,
    strip_recv,
    gather_send,
    gather_recv,
):
    columns, _, height, width = strips.shape
    count = sections * tile_rows
    per_device = gathered.shape[0] // count
    used = columns * QROWS
    groups = height // SUB
    own_images = columns * IMAGES
    section = lax.axis_index("sec")
    tile_row = lax.axis_index("tile")
    me = section * tile_rows + tile_row

    def device(step):
        other = lax.rem(me + step, count)
        return (other // tile_rows, lax.rem(other, tile_rows))

    barrier = pltpu.get_barrier_semaphore()

    @pl.loop(1, count)
    def _(step):
        pl.semaphore_signal(barrier, inc=1, device_id=device(step), device_id_type=MESH)

    local = [
        pltpu.make_async_copy(source, target, local_sem.at[index])
        for index, (source, target) in enumerate(
            (
                (strips_hbm, strips),
                (mask_hbm, mask_ref),
                (offset_hbm, offset_ref),
                (stiff_hbm, stiff_ref),
            )
        )
    ]
    for copy in local:
        copy.start()

    first = lax.broadcasted_iota(jnp.int32, (height, height), 0)
    second = lax.broadcasted_iota(jnp.int32, (height, height), 1)
    gap = second - first
    down = jnp.where(gap == 1, 0.5, jnp.where(gap == -1, -0.5, 0.0)).astype(jnp.bfloat16)
    rows[...] = jnp.zeros_like(rows)

    pl.semaphore_wait(barrier, count - 1)

    def strip_copy(kind, c):
        target = (section, tile_row - 1) if kind == 0 else (section - 1, tile_row)
        return pltpu.make_async_remote_copy(
            src_ref=strips_hbm.at[c, 2 if kind == 0 else 4],
            dst_ref=landed.at[kind, c],
            send_sem=strip_send.at[kind, c],
            recv_sem=strip_recv.at[kind, c],
            device_id=target,
            device_id_type=MESH,
        )

    sends = (tile_row > 0, section > 0)
    receives = (tile_row < tile_rows - 1, section < sections - 1)
    for kind in range(2):

        @pl.when(sends[kind])
        def _():
            for c in range(columns):
                strip_copy(kind, c).start()

    for copy in local:
        copy.wait()

    column = lax.broadcasted_iota(jnp.int32, (height, width), 1)

    def gradients(image, at):
        values = image.astype(jnp.float32)
        before = jnp.where(column == 0, 0.0, pltpu.roll(values, 1, 1))
        after = jnp.where(column == width - 1, 0.0, pltpu.roll(values, width - 1, 1))
        spot = pl.ds(pl.multiple_of(at * height, SUB), height)
        grad_x[spot, :] = (after - before) * 0.5
        grad_y[spot, :] = jnp.dot(down, image, preferred_element_type=jnp.float32)

    def group(ref, image, k):
        return ref[pl.ds(pl.multiple_of(image * height + k * SUB, SUB), SUB), :]

    def put(row, value):
        rows[pl.ds(row, 1), :] = value

    def add(row, value):
        rows[pl.ds(row, 1), :] = rows[pl.ds(row, 1), :] + value

    def exists(c, kind):
        inside = (jnp.int32(c) < columns - 1, receives[0], receives[1])[kind]
        return jnp.where((mask_ref[c, kind] == 1) & inside, 1.0, 0.0)

    def self_blocks(c, image, a_kind, b_kind):
        at = c * IMAGES + image
        gradients(strips[c, image], at)

        def form(k):
            x, y = group(grad_x, at, k), group(grad_y, at, k)
            return (x * x, x * y, y * y)

        base = c * (QROWS * LANES)
        for index, entry in enumerate(column_moments(Products(groups, form), width, True)):
            for moment, value in enumerate(entry):
                spot = index * QUAD + moment
                if a_kind is not None:
                    add(base + SUM_AT + spot, exists(c, a_kind) * value)
                if b_kind is not None:
                    put(base + SELF_AT[b_kind] + spot, value)

    def pair_blocks(kind, c, at_a, at_b, image_a, image_b):
        there = exists(c, kind)
        base = c * (QROWS * LANES)
        for p, ref in enumerate((grad_x, grad_y)):

            def cross(k):
                value = group(ref, at_a, k)
                return (value * group(grad_x, at_b, k), value * group(grad_y, at_b, k))

            for q, entry in enumerate(column_moments(Products(groups, cross), width, True)):
                for moment, value in enumerate(entry):
                    put(base + PAIR_AT[kind] + (2 * p + q) * QUAD + moment, -there * value)

        misfit = image_a.astype(jnp.float32) - image_b.astype(jnp.float32)

        def pulls(k):
            miss = misfit[k * SUB : (k + 1) * SUB]
            return (
                group(grad_x, at_a, k) * miss,
                group(grad_y, at_a, k) * miss,
                group(grad_x, at_b, k) * miss,
                group(grad_y, at_b, k) * miss,
            )

        for index, entry in enumerate(column_moments(Products(groups, pulls), width, False)):
            side, p = divmod(index, 2)
            for weight, value in zip((2, 0, 1), entry):
                if side:
                    put(base + PULL_B_AT + 6 * kind + 3 * p + weight, there * value)
                else:
                    add(base + PULL_A_AT + 3 * p + weight, -there * value)

    @pl.loop(0, columns)
    def _(c):
        self_blocks(c, 4, 2, 2)
        self_blocks(c, 3, 1, None)
        self_blocks(c, 2, None, 1)

    @pl.loop(0, columns - 1)
    def _(c):
        self_blocks(c, 1, 0, None)
        self_blocks(c + 1, 0, None, 0)
        pair_blocks(0, c, c * IMAGES + 1, (c + 1) * IMAGES, strips[c, 1], strips[c + 1, 0])

    ones = jnp.ones((SUB, LANES), jnp.bfloat16)
    lane = lax.broadcasted_iota(jnp.int32, (1, LANES), 1)
    contract = (((1,), (1,)), ((), ()))
    mine = pl.multiple_of(me * per_device, SUB)

    def line_of(c, h):
        part = rows[(c * QROWS + h) * LANES : (c * QROWS + h + 1) * LANES, :]
        high = part.astype(jnp.bfloat16)
        low = (part - high.astype(jnp.float32)).astype(jnp.bfloat16)
        summed = lax.dot_general(ones, high, contract, preferred_element_type=jnp.float32)
        summed = summed + lax.dot_general(ones, low, contract, preferred_element_type=jnp.float32)
        return summed[0:1] * (1.0 / (height * width))

    for c in range(columns):
        line = line_of(c, 0)
        for kind in range(KINDS):
            for axis, extent in ((0, width), (1, height)):
                shift = offset_ref[c, axis, kind].astype(jnp.float32) / extent
                line = jnp.where(lane == OFFSET_AT + 2 * kind + axis, shift, line)
            line = jnp.where(lane == EXISTS_AT + kind, exists(c, kind), line)
        line = jnp.where(lane == STIFF_AT, stiff_ref[c], line)
        gathered[pl.ds(mine + c * QROWS, 1), :] = line

    for kind in (1, 0):

        @pl.when(receives[kind])
        def _():
            @pl.loop(0, columns)
            def _(c):
                strip_copy(kind, c).wait_recv()
                image = ENDS[kind + 1][0]
                at_b = own_images + kind * columns + c
                gradients(landed[kind, c], at_b)
                pair_blocks(
                    kind + 1, c, c * IMAGES + image, at_b, strips[c, image], landed[kind, c]
                )

    for c in range(columns):
        gathered[pl.ds(mine + c * QROWS + 1, 1), :] = line_of(c, 1)

    @pl.loop(1, count)
    def _(step):
        pltpu.make_async_remote_copy(
            src_ref=gathered.at[pl.ds(mine, used)],
            dst_ref=gathered.at[pl.ds(mine, used)],
            send_sem=gather_send,
            recv_sem=gather_recv,
            device_id=device(step),
            device_id_type=MESH,
        ).start()

    others = gathered.at[pl.ds(0, (count - 1) * used)]
    pltpu.make_async_copy(others, others, gather_recv).wait()

    tiles = columns * count
    padded = round_up(tiles, LANES)
    for h in range(QROWS):
        parts = [
            gathered[pl.ds(c * QROWS + h, count, stride=per_device), :] for c in range(columns)
        ]
        if padded > tiles:
            parts.append(jnp.zeros((padded - tiles, LANES), jnp.float32))
        table[h * LANES : (h + 1) * LANES, :] = jnp.concatenate(parts, axis=0).T

    sublane = lax.broadcasted_iota(jnp.int32, (SUB, padded), 0)
    place = lax.broadcasted_iota(jnp.int32, (SUB, padded), 1)
    picks = [sublane == i for i in range(6)]

    def entry(at):
        return table[at : at + 1, :]

    def stacked(spots):
        total = jnp.zeros((SUB, padded), jnp.float32)
        for pick, at in zip(picks, spots):
            total = jnp.where(pick, entry(at), total)
        return total

    def block_at(base, field):
        return [
            stacked(
                [base + field[p][q] * QUAD + MOMENT[a][b] for p in range(2) for a in range(3)]
            )
            for q in range(2)
            for b in range(3)
        ]

    own_field = ((0, 1), (1, 2))
    pair_field = ((0, 1), (2, 3))

    def to_next(array, by):
        return pltpu.roll(array, by, 1)

    def from_next(array, by):
        return pltpu.roll(array, padded - by, 1)

    def shift_rows(vector, offset):
        return vector + offset * jnp.where(sublane < 3, vector[2:3], vector[5:6])

    def shift_columns(block, offset):
        du, dv = offset[0:1], offset[1:2]
        out = []
        for p in range(2):
            last = block[3 * p + 2]
            out += [block[3 * p] + du * last, block[3 * p + 1] + dv * last, last]
        return out

    shifts = (count, 1, tile_rows)
    stiffness = jnp.where(place < tiles, entry(STIFF_AT), 1.0)
    diagonal = [
        column + jnp.where(pick, stiffness, 0.0)
        for pick, column in zip(picks, block_at(SUM_AT, own_field))
    ]
    load = stacked([PULL_A_AT + i for i in range(6)])
    couplings = []
    for kind in range(KINDS):
        by = shifts[kind]
        du, dv = entry(OFFSET_AT + 2 * kind), entry(OFFSET_AT + 2 * kind + 1)
        offset = jnp.where(picks[0] | picks[3], du, jnp.where(picks[1] | picks[4], dv, 0.0))
        offset_b = to_next(offset, by)
        there_b = to_next(jnp.broadcast_to(entry(EXISTS_AT + kind), offset.shape), by)
        block_b = shift_columns(block_at(SELF_AT[kind], own_field), offset_b)
        for j in range(6):
            diagonal[j] = diagonal[j] + there_b * shift_rows(block_b[j], offset_b)
        pull_b = stacked([PULL_B_AT + 6 * kind + i for i in range(6)])
        load = load + to_next(shift_rows(pull_b, offset), by)
        coupling = shift_columns(block_at(PAIR_AT[kind], pair_field), offset)
        couplings.append((coupling, transposed_columns(coupling, sublane), by))

    inverse = inverse_columns(diagonal, sublane)

    def multiply(vector):
        result = apply_columns(diagonal, vector)
        for coupling, flipped, by in couplings:
            result = result + apply_columns(coupling, from_next(vector, by))
            result = result + to_next(apply_columns(flipped, vector), by)
        return result

    def total(array):
        return jnp.sum(jnp.sum(array, axis=0, keepdims=True), axis=1, keepdims=True)

    residual = load
    scaled = apply_columns(inverse, residual)
    product = multiply(scaled)
    rho_now, curve = total(residual * scaled), total(scaled * product)
    step_size = rho_now / curve
    direction, carried = scaled, product
    update = jnp.zeros_like(load)
    for step in range(ITERS):
        update = update + step_size * direction
        residual = residual - step_size * carried
        if step + 1 < ITERS:
            scaled = apply_columns(inverse, residual)
            product = multiply(scaled)
            rho_next, curve = total(residual * scaled), total(scaled * product)
            ratio = rho_next / rho_now
            step_size = rho_next / (curve - ratio * rho_next / step_size)
            direction = scaled + ratio * direction
            carried = product + ratio * carried
            rho_now = rho_next

    turn = sublane[:, :LANES] == place[:, :LANES]
    for index, values in enumerate((update, residual)):
        for c in range(columns):
            own = jnp.sum(jnp.where(place == c * count + me, values, 0.0), axis=1, keepdims=True)
            line = jnp.sum(jnp.where(turn, own, 0.0), axis=0, keepdims=True)
            out_ref[index, c : c + 1, :] = line[:, 0:6]

    pltpu.make_async_copy(others, others, gather_send).wait()
    for kind in range(2):

        @pl.when(sends[kind])
        def _():
            for c in range(columns):
                strip_copy(kind, c).wait_send()


def shards(tile_strips, pair_mask, strip_offset, stiffness):
    _, _, columns, images, height, width = tile_strips.shape
    sections = lax.axis_size("sec")
    tile_rows = lax.axis_size("tile")
    count = sections * tile_rows
    per_device = round_up(columns * QROWS, SUB)
    held = columns * (IMAGES + 2) * height
    padded = round_up(columns * count, LANES)
    both = pl.pallas_call(
        functools.partial(kernel, sections, tile_rows),
        out_shape=jax.ShapeDtypeStruct((2, columns, 6), jnp.float32),
        in_specs=[pl.BlockSpec(memory_space=pltpu.HBM)] * 4,
        out_specs=pl.BlockSpec(memory_space=pltpu.VMEM),
        scratch_shapes=[
            pltpu.VMEM((columns, images, height, width), jnp.bfloat16),
            pltpu.VMEM((2, columns, height, width), jnp.bfloat16),
            pltpu.VMEM((held, width), jnp.float32),
            pltpu.VMEM((held, width), jnp.float32),
            pltpu.VMEM((columns * QROWS * LANES, LANES), jnp.float32),
            pltpu.VMEM((count * per_device, LANES), jnp.float32),
            pltpu.VMEM((QROWS * LANES, padded), jnp.float32),
            pltpu.SMEM((columns, KINDS), jnp.int32),
            pltpu.SMEM((columns, 2, KINDS), jnp.int32),
            pltpu.SMEM((columns,), jnp.float32),
            pltpu.SemaphoreType.DMA((4,)),
            pltpu.SemaphoreType.DMA((2, columns)),
            pltpu.SemaphoreType.DMA((2, columns)),
            pltpu.SemaphoreType.DMA,
            pltpu.SemaphoreType.DMA,
        ],
        compiler_params=pltpu.CompilerParams(
            collective_id=0, has_side_effects=True, vmem_limit_bytes=60 * 1024 * 1024
        ),
    )(
        tile_strips[0, 0],
        pair_mask[0, 0],
        jnp.swapaxes(strip_offset[0, 0], 1, 2),
        stiffness[0, 0],
    )
    both = jnp.swapaxes(both, 1, 2).reshape(2, 6, 1, 1, columns)
    return both[0], both[1]


def solution(mesh):
    return jax.shard_map(
        shards,
        mesh=mesh,
        in_specs=(
            P("sec", "tile", None, None, None, None),
            P("sec", "tile", None, None),
            P("sec", "tile", None, None, None),
            P("sec", "tile", None),
        ),
        out_specs=(P(None, "sec", "tile", None), P(None, "sec", "tile", None)),
        check_vma=False,
    )
```

```python
import functools

import jax
import jax.numpy as jnp
from jax import lax
from jax.experimental import pallas as pl
from jax.experimental.pallas import tpu as pltpu
from jax.sharding import PartitionSpec as P

ITERS = 3
LANES = 128
SUB = 8
IMAGES = 5
KINDS = 3
QROWS = 2
MESH = pl.DeviceIdType.MESH

QUAD = 6
MOMENT = ((3, 4, 1), (4, 5, 2), (1, 2, 0))
SELF = 3 * QUAD
CROSS = 4 * QUAD
SUM_AT = 0
SELF_AT = (SELF, 2 * SELF, 3 * SELF)
OFFSET_AT = 96
EXISTS_AT = 102
STIFF_AT = 105
PAIR_AT = (LANES, LANES + CROSS, LANES + 2 * CROSS)
PULL_A_AT = LANES + 3 * CROSS
PULL_B_AT = PULL_A_AT + 6
ENDS = ((1, 0), (3, 2), (4, 4))


def round_up(value, unit):
    return (value + unit - 1) // unit * unit


def column_moments(fields, width, quadratic):
    groups = fields.groups
    sums = None
    for k in range(groups):
        values = fields(k)
        if sums is None:
            sums = [[value] * (3 if quadratic else 2) for value in values]
        else:
            for entry, value in zip(sums, values):
                entry[0] = entry[0] + value
                entry[1] = entry[1] + entry[0]
                if quadratic:
                    entry[2] = entry[2] + entry[1]
    height = groups * SUB
    step = SUB / height
    row = lax.broadcasted_iota(jnp.int32, (SUB, LANES), 0).astype(jnp.float32)
    column = lax.broadcasted_iota(jnp.int32, (SUB, width), 1).astype(jnp.float32)
    edge = row / height + 0.5
    u = column / width - 0.5

    def fold(array):
        total = array[:, :LANES]
        for start in range(LANES, width, LANES):
            total = total + array[:, start : start + LANES]
        return total

    out = []
    for entry in sums:
        first, second = fold(entry[0]), fold(entry[1])
        scaled = u * entry[0]
        along = fold(scaled)
        moments = [first, along, edge * first - step * second]
        if quadratic:
            third = 2.0 * fold(entry[2]) - second
            moments += [
                fold(u * scaled),
                edge * along - step * fold(u * entry[1]),
                edge * (edge * first - (2.0 * step) * second) + (step * step) * third,
            ]
        out.append([jnp.sum(moment, axis=0, keepdims=True) for moment in moments])
    return out


class Products:
    def __init__(self, groups, form):
        self.groups = groups
        self.form = form

    def __call__(self, k):
        return self.form(k)


def apply_columns(columns, vector):
    total = columns[0] * vector[0:1]
    for j in range(1, 6):
        total = total + columns[j] * vector[j : j + 1]
    return total


def inverse_columns(columns, sublane):
    columns = list(columns)
    for p in range(6):
        pivot = 1.0 / columns[p][p : p + 1]
        here = sublane == p
        lead = columns[p]
        for j in range(6):
            if j != p:
                ratio = columns[j][p : p + 1] * pivot
                columns[j] = jnp.where(here, ratio, columns[j] - lead * ratio)
        columns[p] = jnp.where(here, pivot, -lead * pivot)
    return columns


def transposed_columns(columns, sublane):
    out = []
    for i in range(6):
        total = jnp.zeros_like(columns[0])
        for j in range(6):
            total = jnp.where(sublane == j, columns[j][i : i + 1], total)
        out.append(total)
    return out


def kernel(
    sections,
    tile_rows,
    strips_hbm,
    mask_hbm,
    offset_hbm,
    stiff_hbm,
    out_ref,
    strips,
    landed,
    grad_x,
    grad_y,
    rows,
    gathered,
    table,
    mask_ref,
    offset_ref,
    stiff_ref,
    local_sem,
    strip_send,
    strip_recv,
    gather_send,
    gather_recv,
):
    columns, _, height, width = strips.shape
    count = sections * tile_rows
    per_device = gathered.shape[0] // count
    used = columns * QROWS
    groups = height // SUB
    own_images = columns * IMAGES
    section = lax.axis_index("sec")
    tile_row = lax.axis_index("tile")
    me = section * tile_rows + tile_row

    def device(step):
        other = lax.rem(me + step, count)
        return (other // tile_rows, lax.rem(other, tile_rows))

    barrier = pltpu.get_barrier_semaphore()

    @pl.loop(1, count)
    def _(step):
        pl.semaphore_signal(barrier, inc=1, device_id=device(step), device_id_type=MESH)

    local = [
        pltpu.make_async_copy(source, target, local_sem.at[index])
        for index, (source, target) in enumerate(
            (
                (strips_hbm, strips),
                (mask_hbm, mask_ref),
                (offset_hbm, offset_ref),
                (stiff_hbm, stiff_ref),
            )
        )
    ]
    for copy in local:
        copy.start()

    first = lax.broadcasted_iota(jnp.int32, (height, height), 0)
    second = lax.broadcasted_iota(jnp.int32, (height, height), 1)
    gap = second - first
    down = jnp.where(gap == 1, 0.5, jnp.where(gap == -1, -0.5, 0.0)).astype(jnp.bfloat16)
    rows[...] = jnp.zeros_like(rows)

    pl.semaphore_wait(barrier, count - 1)

    def strip_copy(kind, c):
        target = (section, tile_row - 1) if kind == 0 else (section - 1, tile_row)
        return pltpu.make_async_remote_copy(
            src_ref=strips_hbm.at[c, 2 if kind == 0 else 4],
            dst_ref=landed.at[kind, c],
            send_sem=strip_send.at[kind, c],
            recv_sem=strip_recv.at[kind, c],
            device_id=target,
            device_id_type=MESH,
        )

    sends = (tile_row > 0, section > 0)
    receives = (tile_row < tile_rows - 1, section < sections - 1)
    for kind in range(2):

        @pl.when(sends[kind])
        def _():
            for c in range(columns):
                strip_copy(kind, c).start()

    for copy in local:
        copy.wait()

    column = lax.broadcasted_iota(jnp.int32, (height, width), 1)

    def gradients(image, at):
        values = image.astype(jnp.float32)
        before = jnp.where(column == 0, 0.0, pltpu.roll(values, 1, 1))
        after = jnp.where(column == width - 1, 0.0, pltpu.roll(values, width - 1, 1))
        spot = pl.ds(pl.multiple_of(at * height, SUB), height)
        grad_x[spot, :] = (after - before) * 0.5
        grad_y[spot, :] = jnp.dot(down, image, preferred_element_type=jnp.float32)

    def group(ref, image, k):
        return ref[pl.ds(pl.multiple_of(image * height + k * SUB, SUB), SUB), :]

    def put(row, value):
        rows[pl.ds(row, 1), :] = value

    def add(row, value):
        rows[pl.ds(row, 1), :] = rows[pl.ds(row, 1), :] + value

    def exists(c, kind):
        inside = (jnp.int32(c) < columns - 1, receives[0], receives[1])[kind]
        return jnp.where((mask_ref[c, kind] == 1) & inside, 1.0, 0.0)

    def self_blocks(c, image, a_kind, b_kind):
        at = c * IMAGES + image
        gradients(strips[c, image], at)

        def form(k):
            x, y = group(grad_x, at, k), group(grad_y, at, k)
            return (x * x, x * y, y * y)

        base = c * (QROWS * LANES)
        for index, entry in enumerate(column_moments(Products(groups, form), width, True)):
            for moment, value in enumerate(entry):
                spot = index * QUAD + moment
                if a_kind is not None:
                    add(base + SUM_AT + spot, exists(c, a_kind) * value)
                if b_kind is not None:
                    put(base + SELF_AT[b_kind] + spot, value)

    def pair_blocks(kind, c, at_a, at_b, image_a, image_b):
        there = exists(c, kind)
        base = c * (QROWS * LANES)
        for p, ref in enumerate((grad_x, grad_y)):

            def cross(k):
                value = group(ref, at_a, k)
                return (value * group(grad_x, at_b, k), value * group(grad_y, at_b, k))

            for q, entry in enumerate(column_moments(Products(groups, cross), width, True)):
                for moment, value in enumerate(entry):
                    put(base + PAIR_AT[kind] + (2 * p + q) * QUAD + moment, -there * value)

        misfit = image_a.astype(jnp.float32) - image_b.astype(jnp.float32)

        def pulls(k):
            miss = misfit[k * SUB : (k + 1) * SUB]
            return (
                group(grad_x, at_a, k) * miss,
                group(grad_y, at_a, k) * miss,
                group(grad_x, at_b, k) * miss,
                group(grad_y, at_b, k) * miss,
            )

        for index, entry in enumerate(column_moments(Products(groups, pulls), width, False)):
            side, p = divmod(index, 2)
            for weight, value in zip((2, 0, 1), entry):
                if side:
                    put(base + PULL_B_AT + 6 * kind + 3 * p + weight, there * value)
                else:
                    add(base + PULL_A_AT + 3 * p + weight, -there * value)

    @pl.loop(0, columns)
    def _(c):
        self_blocks(c, 4, 2, 2)
        self_blocks(c, 3, 1, None)
        self_blocks(c, 2, None, 1)

    @pl.loop(0, columns - 1)
    def _(c):
        self_blocks(c, 1, 0, None)
        self_blocks(c + 1, 0, None, 0)
        pair_blocks(0, c, c * IMAGES + 1, (c + 1) * IMAGES, strips[c, 1], strips[c + 1, 0])

    ones = jnp.ones((SUB, LANES), jnp.bfloat16)
    lane = lax.broadcasted_iota(jnp.int32, (1, LANES), 1)
    contract = (((1,), (1,)), ((), ()))
    mine = pl.multiple_of(me * per_device, SUB)

    def line_of(c, h):
        part = rows[(c * QROWS + h) * LANES : (c * QROWS + h + 1) * LANES, :]
        high = part.astype(jnp.bfloat16)
        low = (part - high.astype(jnp.float32)).astype(jnp.bfloat16)
        summed = lax.dot_general(ones, high, contract, preferred_element_type=jnp.float32)
        summed = summed + lax.dot_general(ones, low, contract, preferred_element_type=jnp.float32)
        return summed[0:1] * (1.0 / (height * width))

    for c in range(columns):
        line = line_of(c, 0)
        for kind in range(KINDS):
            for axis, extent in ((0, width), (1, height)):
                shift = offset_ref[c, axis, kind].astype(jnp.float32) / extent
                line = jnp.where(lane == OFFSET_AT + 2 * kind + axis, shift, line)
            line = jnp.where(lane == EXISTS_AT + kind, exists(c, kind), line)
        line = jnp.where(lane == STIFF_AT, stiff_ref[c], line)
        gathered[pl.ds(mine + c * QROWS, 1), :] = line

    for kind in (1, 0):

        @pl.when(receives[kind])
        def _():
            @pl.loop(0, columns)
            def _(c):
                strip_copy(kind, c).wait_recv()
                image = ENDS[kind + 1][0]
                at_b = own_images + kind * columns + c
                gradients(landed[kind, c], at_b)
                pair_blocks(
                    kind + 1, c, c * IMAGES + image, at_b, strips[c, image], landed[kind, c]
                )

    for c in range(columns):
        gathered[pl.ds(mine + c * QROWS + 1, 1), :] = line_of(c, 1)

    @pl.loop(1, count)
    def _(step):
        pltpu.make_async_remote_copy(
            src_ref=gathered.at[pl.ds(mine, used)],
            dst_ref=gathered.at[pl.ds(mine, used)],
            send_sem=gather_send,
            recv_sem=gather_recv,
            device_id=device(step),
            device_id_type=MESH,
        ).start()

    others = gathered.at[pl.ds(0, (count - 1) * used)]
    pltpu.make_async_copy(others, others, gather_recv).wait()

    tiles = columns * count
    padded = round_up(tiles, LANES)
    for h in range(QROWS):
        parts = [
            gathered[pl.ds(c * QROWS + h, count, stride=per_device), :] for c in range(columns)
        ]
        if padded > tiles:
            parts.append(jnp.zeros((padded - tiles, LANES), jnp.float32))
        table[h * LANES : (h + 1) * LANES, :] = jnp.concatenate(parts, axis=0).T

    sublane = lax.broadcasted_iota(jnp.int32, (SUB, padded), 0)
    place = lax.broadcasted_iota(jnp.int32, (SUB, padded), 1)
    picks = [sublane == i for i in range(6)]

    def entry(at):
        return table[at : at + 1, :]

    def stacked(spots):
        total = jnp.zeros((SUB, padded), jnp.float32)
        for pick, at in zip(picks, spots):
            total = jnp.where(pick, entry(at), total)
        return total

    def block_at(base, field):
        return [
            stacked(
                [base + field[p][q] * QUAD + MOMENT[a][b] for p in range(2) for a in range(3)]
            )
            for q in range(2)
            for b in range(3)
        ]

    own_field = ((0, 1), (1, 2))
    pair_field = ((0, 1), (2, 3))

    def to_next(array, by):
        return pltpu.roll(array, by, 1)

    def from_next(array, by):
        return pltpu.roll(array, padded - by, 1)

    def shift_rows(vector, offset):
        return vector + offset * jnp.where(sublane < 3, vector[2:3], vector[5:6])

    def shift_columns(block, offset):
        du, dv = offset[0:1], offset[1:2]
        out = []
        for p in range(2):
            last = block[3 * p + 2]
            out += [block[3 * p] + du * last, block[3 * p + 1] + dv * last, last]
        return out

    shifts = (count, 1, tile_rows)
    stiffness = jnp.where(place < tiles, entry(STIFF_AT), 1.0)
    diagonal = [
        column + jnp.where(pick, stiffness, 0.0)
        for pick, column in zip(picks, block_at(SUM_AT, own_field))
    ]
    load = stacked([PULL_A_AT + i for i in range(6)])
    couplings = []
    for kind in range(KINDS):
        by = shifts[kind]
        du, dv = entry(OFFSET_AT + 2 * kind), entry(OFFSET_AT + 2 * kind + 1)
        offset = jnp.where(picks[0] | picks[3], du, jnp.where(picks[1] | picks[4], dv, 0.0))
        offset_b = to_next(offset, by)
        there_b = to_next(jnp.broadcast_to(entry(EXISTS_AT + kind), offset.shape), by)
        block_b = shift_columns(block_at(SELF_AT[kind], own_field), offset_b)
        for j in range(6):
            diagonal[j] = diagonal[j] + there_b * shift_rows(block_b[j], offset_b)
        pull_b = stacked([PULL_B_AT + 6 * kind + i for i in range(6)])
        load = load + to_next(shift_rows(pull_b, offset), by)
        coupling = shift_columns(block_at(PAIR_AT[kind], pair_field), offset)
        couplings.append((coupling, transposed_columns(coupling, sublane), by))

    inverse = inverse_columns(diagonal, sublane)

    def multiply(vector):
        result = apply_columns(diagonal, vector)
        for coupling, flipped, by in couplings:
            result = result + apply_columns(coupling, from_next(vector, by))
            result = result + to_next(apply_columns(flipped, vector), by)
        return result

    def total(array):
        return jnp.sum(jnp.sum(array, axis=0, keepdims=True), axis=1, keepdims=True)

    residual = load
    scaled = apply_columns(inverse, residual)
    product = multiply(scaled)
    rho_now, curve = total(residual * scaled), total(scaled * product)
    step_size = rho_now / curve
    direction, carried = scaled, product
    update = jnp.zeros_like(load)
    for step in range(ITERS):
        update = update + step_size * direction
        residual = residual - step_size * carried
        if step + 1 < ITERS:
            scaled = apply_columns(inverse, residual)
            product = multiply(scaled)
            rho_next, curve = total(residual * scaled), total(scaled * product)
            ratio = rho_next / rho_now
            step_size = rho_next / (curve - ratio * rho_next / step_size)
            direction = scaled + ratio * direction
            carried = product + ratio * carried
            rho_now = rho_next

    turn = sublane[:, :LANES] == place[:, :LANES]
    for index, values in enumerate((update, residual)):
        for c in range(columns):
            own = jnp.sum(jnp.where(place == c * count + me, values, 0.0), axis=1, keepdims=True)
            line = jnp.sum(jnp.where(turn, own, 0.0), axis=0, keepdims=True)
            out_ref[index, c : c + 1, :] = line[:, 0:6]

    pltpu.make_async_copy(others, others, gather_send).wait()
    for kind in range(2):

        @pl.when(sends[kind])
        def _():
            for c in range(columns):
                strip_copy(kind, c).wait_send()


def shards(tile_strips, pair_mask, strip_offset, stiffness):
    _, _, columns, images, height, width = tile_strips.shape
    sections = lax.axis_size("sec")
    tile_rows = lax.axis_size("tile")
    count = sections * tile_rows
    per_device = round_up(columns * QROWS, SUB)
    held = columns * (IMAGES + 2) * height
    padded = round_up(columns * count, LANES)
    both = pl.pallas_call(
        functools.partial(kernel, sections, tile_rows),
        out_shape=jax.ShapeDtypeStruct((2, columns, 6), jnp.float32),
        in_specs=[pl.BlockSpec(memory_space=pltpu.HBM)] * 4,
        out_specs=pl.BlockSpec(memory_space=pltpu.VMEM),
        scratch_shapes=[
            pltpu.VMEM((columns, images, height, width), jnp.bfloat16),
            pltpu.VMEM((2, columns, height, width), jnp.bfloat16),
            pltpu.VMEM((held, width), jnp.float32),
            pltpu.VMEM((held, width), jnp.float32),
            pltpu.VMEM((columns * QROWS * LANES, LANES), jnp.float32),
            pltpu.VMEM((count * per_device, LANES), jnp.float32),
            pltpu.VMEM((QROWS * LANES, padded), jnp.float32),
            pltpu.SMEM((columns, KINDS), jnp.int32),
            pltpu.SMEM((columns, 2, KINDS), jnp.int32),
            pltpu.SMEM((columns,), jnp.float32),
            pltpu.SemaphoreType.DMA((4,)),
            pltpu.SemaphoreType.DMA((2, columns)),
            pltpu.SemaphoreType.DMA((2, columns)),
            pltpu.SemaphoreType.DMA,
            pltpu.SemaphoreType.DMA,
        ],
        compiler_params=pltpu.CompilerParams(
            collective_id=0, has_side_effects=True, vmem_limit_bytes=60 * 1024 * 1024
        ),
    )(
        tile_strips[0, 0],
        pair_mask[0, 0],
        jnp.swapaxes(strip_offset[0, 0], 1, 2),
        stiffness[0, 0],
    )
    both = jnp.swapaxes(both, 1, 2).reshape(2, 6, 1, 1, columns)
    return both[0], both[1]


def solution(mesh):
    return jax.shard_map(
        shards,
        mesh=mesh,
        in_specs=(
            P("sec", "tile", None, None, None, None),
            P("sec", "tile", None, None),
            P("sec", "tile", None, None, None),
            P("sec", "tile", None),
        ),
        out_specs=(P(None, "sec", "tile", None), P(None, "sec", "tile", None)),
        check_vma=False,
    )
```

```python
import functools

import jax
import jax.numpy as jnp
from jax import lax
from jax.experimental import pallas as pl
from jax.experimental.pallas import tpu as pltpu
from jax.sharding import PartitionSpec as P

ITERS = 3
LANES = 128
SUB = 8
IMAGES = 5
KINDS = 3
QROWS = 2
MESH = pl.DeviceIdType.MESH

QUAD = 6
MOMENT = ((3, 4, 1), (4, 5, 2), (1, 2, 0))
SELF = 3 * QUAD
CROSS = 4 * QUAD
SUM_AT = 0
SELF_AT = (SELF, 2 * SELF, 3 * SELF)
OFFSET_AT = 96
EXISTS_AT = 102
STIFF_AT = 105
PAIR_AT = (LANES, LANES + CROSS, LANES + 2 * CROSS)
PULL_A_AT = LANES + 3 * CROSS
PULL_B_AT = PULL_A_AT + 6
ENDS = ((1, 0), (3, 2), (4, 4))


def round_up(value, unit):
    return (value + unit - 1) // unit * unit


def column_moments(fields, width, quadratic):
    groups = fields.groups
    sums = None
    for k in range(groups):
        values = fields(k)
        if sums is None:
            sums = [[value] * (3 if quadratic else 2) for value in values]
        else:
            for entry, value in zip(sums, values):
                entry[0] = entry[0] + value
                entry[1] = entry[1] + entry[0]
                if quadratic:
                    entry[2] = entry[2] + entry[1]
    height = groups * SUB
    step = SUB / height
    row = lax.broadcasted_iota(jnp.int32, (SUB, LANES), 0).astype(jnp.float32)
    column = lax.broadcasted_iota(jnp.int32, (SUB, width), 1).astype(jnp.float32)
    edge = row / height + 0.5
    u = column / width - 0.5

    def fold(array):
        total = array[:, :LANES]
        for start in range(LANES, width, LANES):
            total = total + array[:, start : start + LANES]
        return total

    out = []
    for entry in sums:
        first, second = fold(entry[0]), fold(entry[1])
        scaled = u * entry[0]
        along = fold(scaled)
        moments = [first, along, edge * first - step * second]
        if quadratic:
            third = 2.0 * fold(entry[2]) - second
            moments += [
                fold(u * scaled),
                edge * along - step * fold(u * entry[1]),
                edge * (edge * first - (2.0 * step) * second) + (step * step) * third,
            ]
        out.append([jnp.sum(moment, axis=0, keepdims=True) for moment in moments])
    return out


class Products:
    def __init__(self, groups, form):
        self.groups = groups
        self.form = form

    def __call__(self, k):
        return self.form(k)


def apply_columns(columns, vector):
    total = columns[0] * vector[0:1]
    for j in range(1, 6):
        total = total + columns[j] * vector[j : j + 1]
    return total


def inverse_columns(columns, sublane):
    columns = list(columns)
    for p in range(6):
        pivot = 1.0 / columns[p][p : p + 1]
        here = sublane == p
        lead = columns[p]
        for j in range(6):
            if j != p:
                ratio = columns[j][p : p + 1] * pivot
                columns[j] = jnp.where(here, ratio, columns[j] - lead * ratio)
        columns[p] = jnp.where(here, pivot, -lead * pivot)
    return columns


def transposed_columns(columns, sublane):
    out = []
    for i in range(6):
        total = jnp.zeros_like(columns[0])
        for j in range(6):
            total = jnp.where(sublane == j, columns[j][i : i + 1], total)
        out.append(total)
    return out


def kernel(
    sections,
    tile_rows,
    strips_hbm,
    mask_hbm,
    offset_hbm,
    stiff_hbm,
    out_ref,
    strips,
    landed,
    grad_x,
    grad_y,
    rows,
    gathered,
    table,
    mask_ref,
    offset_ref,
    stiff_ref,
    local_sem,
    strip_send,
    strip_recv,
    gather_send,
    gather_recv,
):
    columns, _, height, width = strips.shape
    count = sections * tile_rows
    used = columns * QROWS
    groups = height // SUB
    own_images = columns * IMAGES
    section = lax.axis_index("sec")
    tile_row = lax.axis_index("tile")
    me = section * tile_rows + tile_row

    def along_tile(step):
        return (section, lax.rem(tile_row + step, tile_rows))

    def along_sec(step):
        return (lax.rem(section + step, sections), tile_row)

    barrier = pltpu.get_barrier_semaphore()

    for size, device in ((tile_rows, along_tile), (sections, along_sec)):

        @pl.loop(1, size)
        def _(step):
            pl.semaphore_signal(barrier, inc=1, device_id=device(step), device_id_type=MESH)

    local = [
        pltpu.make_async_copy(source, target, local_sem.at[index])
        for index, (source, target) in enumerate(
            (
                (strips_hbm, strips),
                (mask_hbm, mask_ref),
                (offset_hbm, offset_ref),
                (stiff_hbm, stiff_ref),
            )
        )
    ]
    for copy in local:
        copy.start()

    first = lax.broadcasted_iota(jnp.int32, (height, height), 0)
    second = lax.broadcasted_iota(jnp.int32, (height, height), 1)
    gap = second - first
    down = jnp.where(gap == 1, 0.5, jnp.where(gap == -1, -0.5, 0.0)).astype(jnp.bfloat16)
    rows[...] = jnp.zeros_like(rows)

    pl.semaphore_wait(barrier, tile_rows + sections - 2)

    def strip_copy(kind, c):
        target = (section, tile_row - 1) if kind == 0 else (section - 1, tile_row)
        return pltpu.make_async_remote_copy(
            src_ref=strips_hbm.at[c, 2 if kind == 0 else 4],
            dst_ref=landed.at[kind, c],
            send_sem=strip_send.at[kind, c],
            recv_sem=strip_recv.at[kind, c],
            device_id=target,
            device_id_type=MESH,
        )

    sends = (tile_row > 0, section > 0)
    receives = (tile_row < tile_rows - 1, section < sections - 1)
    for kind in range(2):

        @pl.when(sends[kind])
        def _():
            for c in range(columns):
                strip_copy(kind, c).start()

    for copy in local:
        copy.wait()

    column = lax.broadcasted_iota(jnp.int32, (height, width), 1)

    def gradients(image, at):
        values = image.astype(jnp.float32)
        before = jnp.where(column == 0, 0.0, pltpu.roll(values, 1, 1))
        after = jnp.where(column == width - 1, 0.0, pltpu.roll(values, width - 1, 1))
        spot = pl.ds(pl.multiple_of(at * height, SUB), height)
        grad_x[spot, :] = (after - before) * 0.5
        grad_y[spot, :] = jnp.dot(down, image, preferred_element_type=jnp.float32)

    def group(ref, image, k):
        return ref[pl.ds(pl.multiple_of(image * height + k * SUB, SUB), SUB), :]

    def put(row, value):
        rows[pl.ds(row, 1), :] = value

    def add(row, value):
        rows[pl.ds(row, 1), :] = rows[pl.ds(row, 1), :] + value

    def exists(c, kind):
        inside = (jnp.int32(c) < columns - 1, receives[0], receives[1])[kind]
        return jnp.where((mask_ref[c, kind] == 1) & inside, 1.0, 0.0)

    def self_blocks(c, image, a_kind, b_kind):
        at = c * IMAGES + image
        gradients(strips[c, image], at)

        def form(k):
            x, y = group(grad_x, at, k), group(grad_y, at, k)
            return (x * x, x * y, y * y)

        base = c * (QROWS * LANES)
        for index, entry in enumerate(column_moments(Products(groups, form), width, True)):
            for moment, value in enumerate(entry):
                spot = index * QUAD + moment
                if a_kind is not None:
                    add(base + SUM_AT + spot, exists(c, a_kind) * value)
                if b_kind is not None:
                    put(base + SELF_AT[b_kind] + spot, value)

    def pair_blocks(kind, c, at_a, at_b, image_a, image_b):
        there = exists(c, kind)
        base = c * (QROWS * LANES)
        for p, ref in enumerate((grad_x, grad_y)):

            def cross(k):
                value = group(ref, at_a, k)
                return (value * group(grad_x, at_b, k), value * group(grad_y, at_b, k))

            for q, entry in enumerate(column_moments(Products(groups, cross), width, True)):
                for moment, value in enumerate(entry):
                    put(base + PAIR_AT[kind] + (2 * p + q) * QUAD + moment, -there * value)

        misfit = image_a.astype(jnp.float32) - image_b.astype(jnp.float32)

        def pulls(k):
            miss = misfit[k * SUB : (k + 1) * SUB]
            return (
                group(grad_x, at_a, k) * miss,
                group(grad_y, at_a, k) * miss,
                group(grad_x, at_b, k) * miss,
                group(grad_y, at_b, k) * miss,
            )

        for index, entry in enumerate(column_moments(Products(groups, pulls), width, False)):
            side, p = divmod(index, 2)
            for weight, value in zip((2, 0, 1), entry):
                if side:
                    put(base + PULL_B_AT + 6 * kind + 3 * p + weight, there * value)
                else:
                    add(base + PULL_A_AT + 3 * p + weight, -there * value)

    @pl.loop(0, columns)
    def _(c):
        self_blocks(c, 4, 2, 2)
        self_blocks(c, 3, 1, None)
        self_blocks(c, 2, None, 1)

    @pl.loop(0, columns - 1)
    def _(c):
        self_blocks(c, 1, 0, None)
        self_blocks(c + 1, 0, None, 0)
        pair_blocks(0, c, c * IMAGES + 1, (c + 1) * IMAGES, strips[c, 1], strips[c + 1, 0])

    ones = jnp.ones((SUB, LANES), jnp.bfloat16)
    lane = lax.broadcasted_iota(jnp.int32, (1, LANES), 1)
    contract = (((1,), (1,)), ((), ()))

    def line_of(c, h):
        part = rows[(c * QROWS + h) * LANES : (c * QROWS + h + 1) * LANES, :]
        high = part.astype(jnp.bfloat16)
        low = (part - high.astype(jnp.float32)).astype(jnp.bfloat16)
        summed = lax.dot_general(ones, high, contract, preferred_element_type=jnp.float32)
        summed = summed + lax.dot_general(ones, low, contract, preferred_element_type=jnp.float32)
        return summed[0:1] * (1.0 / (height * width))

    for c in range(columns):
        line = line_of(c, 0)
        for kind in range(KINDS):
            for axis, extent in ((0, width), (1, height)):
                shift = offset_ref[c, axis, kind].astype(jnp.float32) / extent
                line = jnp.where(lane == OFFSET_AT + 2 * kind + axis, shift, line)
            line = jnp.where(lane == EXISTS_AT + kind, exists(c, kind), line)
        line = jnp.where(lane == STIFF_AT, stiff_ref[c], line)
        gathered[me, c * QROWS : c * QROWS + 1, :] = line

    for kind in (1, 0):

        @pl.when(receives[kind])
        def _():
            @pl.loop(0, columns)
            def _(c):
                strip_copy(kind, c).wait_recv()
                image = ENDS[kind + 1][0]
                at_b = own_images + kind * columns + c
                gradients(landed[kind, c], at_b)
                pair_blocks(
                    kind + 1, c, c * IMAGES + image, at_b, strips[c, image], landed[kind, c]
                )

    for c in range(columns):
        gathered[me, c * QROWS + 1 : c * QROWS + 2, :] = line_of(c, 1)

    def slots(start, length):
        return gathered.at[pl.ds(start, length), pl.ds(0, used)]

    stages = (
        (tile_rows, along_tile, me, 1),
        (sections, along_sec, section * tile_rows, tile_rows),
    )
    for stage, (size, device, start, length) in enumerate(stages):

        @pl.loop(1, size)
        def _(step):
            pltpu.make_async_remote_copy(
                src_ref=slots(start, length),
                dst_ref=slots(start, length),
                send_sem=gather_send.at[stage],
                recv_sem=gather_recv.at[stage],
                device_id=device(step),
                device_id_type=MESH,
            ).start()

        others = slots(0, (size - 1) * length)
        pltpu.make_async_copy(others, others, gather_recv.at[stage]).wait()

    tiles = columns * count
    padded = round_up(tiles, LANES)
    for h in range(QROWS):
        parts = [
            gathered[:, c * QROWS + h, :] for c in range(columns)
        ]
        if padded > tiles:
            parts.append(jnp.zeros((padded - tiles, LANES), jnp.float32))
        table[h * LANES : (h + 1) * LANES, :] = jnp.concatenate(parts, axis=0).T

    sublane = lax.broadcasted_iota(jnp.int32, (SUB, padded), 0)
    place = lax.broadcasted_iota(jnp.int32, (SUB, padded), 1)
    picks = [sublane == i for i in range(6)]

    def entry(at):
        return table[at : at + 1, :]

    def stacked(spots):
        total = jnp.zeros((SUB, padded), jnp.float32)
        for pick, at in zip(picks, spots):
            total = jnp.where(pick, entry(at), total)
        return total

    def block_at(base, field):
        return [
            stacked(
                [base + field[p][q] * QUAD + MOMENT[a][b] for p in range(2) for a in range(3)]
            )
            for q in range(2)
            for b in range(3)
        ]

    own_field = ((0, 1), (1, 2))
    pair_field = ((0, 1), (2, 3))

    def to_next(array, by):
        return pltpu.roll(array, by, 1)

    def from_next(array, by):
        return pltpu.roll(array, padded - by, 1)

    def shift_rows(vector, offset):
        return vector + offset * jnp.where(sublane < 3, vector[2:3], vector[5:6])

    def shift_columns(block, offset):
        du, dv = offset[0:1], offset[1:2]
        out = []
        for p in range(2):
            last = block[3 * p + 2]
            out += [block[3 * p] + du * last, block[3 * p + 1] + dv * last, last]
        return out

    shifts = (count, 1, tile_rows)
    stiffness = jnp.where(place < tiles, entry(STIFF_AT), 1.0)
    diagonal = [
        column + jnp.where(pick, stiffness, 0.0)
        for pick, column in zip(picks, block_at(SUM_AT, own_field))
    ]
    load = stacked([PULL_A_AT + i for i in range(6)])
    couplings = []
    for kind in range(KINDS):
        by = shifts[kind]
        du, dv = entry(OFFSET_AT + 2 * kind), entry(OFFSET_AT + 2 * kind + 1)
        offset = jnp.where(picks[0] | picks[3], du, jnp.where(picks[1] | picks[4], dv, 0.0))
        offset_b = to_next(offset, by)
        there_b = to_next(jnp.broadcast_to(entry(EXISTS_AT + kind), offset.shape), by)
        block_b = shift_columns(block_at(SELF_AT[kind], own_field), offset_b)
        for j in range(6):
            diagonal[j] = diagonal[j] + there_b * shift_rows(block_b[j], offset_b)
        pull_b = stacked([PULL_B_AT + 6 * kind + i for i in range(6)])
        load = load + to_next(shift_rows(pull_b, offset), by)
        coupling = shift_columns(block_at(PAIR_AT[kind], pair_field), offset)
        couplings.append((coupling, transposed_columns(coupling, sublane), by))

    inverse = inverse_columns(diagonal, sublane)

    def multiply(vector):
        result = apply_columns(diagonal, vector)
        for coupling, flipped, by in couplings:
            result = result + apply_columns(coupling, from_next(vector, by))
            result = result + to_next(apply_columns(flipped, vector), by)
        return result

    def total(array):
        return jnp.sum(jnp.sum(array, axis=0, keepdims=True), axis=1, keepdims=True)

    residual = load
    scaled = apply_columns(inverse, residual)
    product = multiply(scaled)
    rho_now, curve = total(residual * scaled), total(scaled * product)
    step_size = rho_now / curve
    direction, carried = scaled, product
    update = jnp.zeros_like(load)
    for step in range(ITERS):
        update = update + step_size * direction
        residual = residual - step_size * carried
        if step + 1 < ITERS:
            scaled = apply_columns(inverse, residual)
            product = multiply(scaled)
            rho_next, curve = total(residual * scaled), total(scaled * product)
            ratio = rho_next / rho_now
            step_size = rho_next / (curve - ratio * rho_next / step_size)
            direction = scaled + ratio * direction
            carried = product + ratio * carried
            rho_now = rho_next

    turn = sublane[:, :LANES] == place[:, :LANES]
    for index, values in enumerate((update, residual)):
        for c in range(columns):
            own = jnp.sum(jnp.where(place == c * count + me, values, 0.0), axis=1, keepdims=True)
            line = jnp.sum(jnp.where(turn, own, 0.0), axis=0, keepdims=True)
            out_ref[index, c : c + 1, :] = line[:, 0:6]

    for stage, (size, _, _, length) in enumerate(stages):
        others = slots(0, (size - 1) * length)
        pltpu.make_async_copy(others, others, gather_send.at[stage]).wait()
    for kind in range(2):

        @pl.when(sends[kind])
        def _():
            for c in range(columns):
                strip_copy(kind, c).wait_send()


def shards(tile_strips, pair_mask, strip_offset, stiffness):
    _, _, columns, images, height, width = tile_strips.shape
    sections = lax.axis_size("sec")
    tile_rows = lax.axis_size("tile")
    count = sections * tile_rows
    per_device = round_up(columns * QROWS, SUB)
    held = columns * (IMAGES + 2) * height
    padded = round_up(columns * count, LANES)
    both = pl.pallas_call(
        functools.partial(kernel, sections, tile_rows),
        out_shape=jax.ShapeDtypeStruct((2, columns, 6), jnp.float32),
        in_specs=[pl.BlockSpec(memory_space=pltpu.HBM)] * 4,
        out_specs=pl.BlockSpec(memory_space=pltpu.VMEM),
        scratch_shapes=[
            pltpu.VMEM((columns, images, height, width), jnp.bfloat16),
            pltpu.VMEM((2, columns, height, width), jnp.bfloat16),
            pltpu.VMEM((held, width), jnp.float32),
            pltpu.VMEM((held, width), jnp.float32),
            pltpu.VMEM((columns * QROWS * LANES, LANES), jnp.float32),
            pltpu.VMEM((count, per_device, LANES), jnp.float32),
            pltpu.VMEM((QROWS * LANES, padded), jnp.float32),
            pltpu.SMEM((columns, KINDS), jnp.int32),
            pltpu.SMEM((columns, 2, KINDS), jnp.int32),
            pltpu.SMEM((columns,), jnp.float32),
            pltpu.SemaphoreType.DMA((4,)),
            pltpu.SemaphoreType.DMA((2, columns)),
            pltpu.SemaphoreType.DMA((2, columns)),
            pltpu.SemaphoreType.DMA((2,)),
            pltpu.SemaphoreType.DMA((2,)),
        ],
        compiler_params=pltpu.CompilerParams(
            collective_id=0, has_side_effects=True, vmem_limit_bytes=54784 * 1024
        ),
    )(
        tile_strips[0, 0],
        pair_mask[0, 0],
        jnp.swapaxes(strip_offset[0, 0], 1, 2),
        stiffness[0, 0],
    )
    both = jnp.swapaxes(both, 1, 2).reshape(2, 6, 1, 1, columns)
    return both[0], both[1]


def solution(mesh):
    return jax.shard_map(
        shards,
        mesh=mesh,
        in_specs=(
            P("sec", "tile", None, None, None, None),
            P("sec", "tile", None, None),
            P("sec", "tile", None, None, None),
            P("sec", "tile", None),
        ),
        out_specs=(P(None, "sec", "tile", None), P(None, "sec", "tile", None)),
        check_vma=False,
    )
```

```python
import functools

import jax
import jax.numpy as jnp
from jax import lax
from jax.experimental import pallas as pl
from jax.experimental.pallas import tpu as pltpu
from jax.sharding import PartitionSpec as P

ITERS = 3
LANES = 128
SUB = 8
IMAGES = 5
KINDS = 3
QROWS = 2
MESH = pl.DeviceIdType.MESH

QUAD = 6
MOMENT = ((3, 4, 1), (4, 5, 2), (1, 2, 0))
SELF = 3 * QUAD
CROSS = 4 * QUAD
SUM_AT = 0
SELF_AT = (SELF, 2 * SELF, 3 * SELF)
OFFSET_AT = 96
EXISTS_AT = 102
STIFF_AT = 105
PAIR_AT = (LANES, LANES + CROSS, LANES + 2 * CROSS)
PULL_A_AT = LANES + 3 * CROSS
PULL_B_AT = PULL_A_AT + 6
ENDS = ((1, 0), (3, 2), (4, 4))


def round_up(value, unit):
    return (value + unit - 1) // unit * unit


def column_moments(fields, width, quadratic):
    groups = fields.groups
    sums = None
    for k in range(groups):
        values = fields(k)
        if sums is None:
            sums = [[value] * (3 if quadratic else 2) for value in values]
        else:
            for entry, value in zip(sums, values):
                entry[0] = entry[0] + value
                entry[1] = entry[1] + entry[0]
                if quadratic:
                    entry[2] = entry[2] + entry[1]
    height = groups * SUB
    step = SUB / height
    row = lax.broadcasted_iota(jnp.int32, (SUB, LANES), 0).astype(jnp.float32)
    column = lax.broadcasted_iota(jnp.int32, (SUB, width), 1).astype(jnp.float32)
    edge = row / height + 0.5
    u = column / width - 0.5

    def fold(array):
        total = array[:, :LANES]
        for start in range(LANES, width, LANES):
            total = total + array[:, start : start + LANES]
        return total

    out = []
    for entry in sums:
        first, second = fold(entry[0]), fold(entry[1])
        scaled = u * entry[0]
        along = fold(scaled)
        moments = [first, along, edge * first - step * second]
        if quadratic:
            third = 2.0 * fold(entry[2]) - second
            moments += [
                fold(u * scaled),
                edge * along - step * fold(u * entry[1]),
                edge * (edge * first - (2.0 * step) * second) + (step * step) * third,
            ]
        out.append([jnp.sum(moment, axis=0, keepdims=True) for moment in moments])
    return out


class Products:
    def __init__(self, groups, form):
        self.groups = groups
        self.form = form

    def __call__(self, k):
        return self.form(k)


def apply_columns(columns, vector):
    total = columns[0] * vector[0:1]
    for j in range(1, 6):
        total = total + columns[j] * vector[j : j + 1]
    return total


def inverse_columns(columns, sublane):
    columns = list(columns)
    for p in range(6):
        pivot = 1.0 / columns[p][p : p + 1]
        here = sublane == p
        lead = columns[p]
        for j in range(6):
            if j != p:
                ratio = columns[j][p : p + 1] * pivot
                columns[j] = jnp.where(here, ratio, columns[j] - lead * ratio)
        columns[p] = jnp.where(here, pivot, -lead * pivot)
    return columns


def transposed_columns(columns, sublane):
    out = []
    for i in range(6):
        total = jnp.zeros_like(columns[0])
        for j in range(6):
            total = jnp.where(sublane == j, columns[j][i : i + 1], total)
        out.append(total)
    return out


def kernel(
    sections,
    tile_rows,
    strips_hbm,
    mask_hbm,
    offset_hbm,
    stiff_hbm,
    out_ref,
    strips,
    landed,
    grad_x,
    grad_y,
    rows,
    early,
    late,
    table,
    mask_ref,
    offset_ref,
    stiff_ref,
    local_sem,
    strip_send,
    strip_recv,
    gather_send,
    gather_recv,
):
    columns, _, height, width = strips.shape
    count = sections * tile_rows
    per_device = early.shape[0] // count
    groups = height // SUB
    own_images = columns * IMAGES
    section = lax.axis_index("sec")
    tile_row = lax.axis_index("tile")
    me = section * tile_rows + tile_row

    def device(step):
        other = lax.rem(me + step, count)
        return (other // tile_rows, lax.rem(other, tile_rows))

    barrier = pltpu.get_barrier_semaphore()

    @pl.loop(1, count)
    def _(step):
        pl.semaphore_signal(barrier, inc=1, device_id=device(step), device_id_type=MESH)

    local = [
        pltpu.make_async_copy(source, target, local_sem.at[index])
        for index, (source, target) in enumerate(
            (
                (strips_hbm, strips),
                (mask_hbm, mask_ref),
                (offset_hbm, offset_ref),
                (stiff_hbm, stiff_ref),
            )
        )
    ]
    for copy in local:
        copy.start()

    first = lax.broadcasted_iota(jnp.int32, (height, height), 0)
    second = lax.broadcasted_iota(jnp.int32, (height, height), 1)
    gap = second - first
    down = jnp.where(gap == 1, 0.5, jnp.where(gap == -1, -0.5, 0.0)).astype(jnp.bfloat16)
    rows[...] = jnp.zeros_like(rows)

    pl.semaphore_wait(barrier, count - 1)

    def strip_copy(kind, c):
        target = (section, tile_row - 1) if kind == 0 else (section - 1, tile_row)
        return pltpu.make_async_remote_copy(
            src_ref=strips_hbm.at[c, 2 if kind == 0 else 4],
            dst_ref=landed.at[kind, c],
            send_sem=strip_send.at[kind, c],
            recv_sem=strip_recv.at[kind, c],
            device_id=target,
            device_id_type=MESH,
        )

    sends = (tile_row > 0, section > 0)
    receives = (tile_row < tile_rows - 1, section < sections - 1)
    for kind in range(2):

        @pl.when(sends[kind])
        def _():
            for c in range(columns):
                strip_copy(kind, c).start()

    for copy in local:
        copy.wait()

    column = lax.broadcasted_iota(jnp.int32, (height, width), 1)

    def gradients(image, at):
        values = image.astype(jnp.float32)
        before = jnp.where(column == 0, 0.0, pltpu.roll(values, 1, 1))
        after = jnp.where(column == width - 1, 0.0, pltpu.roll(values, width - 1, 1))
        spot = pl.ds(pl.multiple_of(at * height, SUB), height)
        grad_x[spot, :] = (after - before) * 0.5
        grad_y[spot, :] = jnp.dot(down, image, preferred_element_type=jnp.float32)

    def group(ref, image, k):
        return ref[pl.ds(pl.multiple_of(image * height + k * SUB, SUB), SUB), :]

    def put(row, value):
        rows[pl.ds(row, 1), :] = value

    def add(row, value):
        rows[pl.ds(row, 1), :] = rows[pl.ds(row, 1), :] + value

    def exists(c, kind):
        inside = (jnp.int32(c) < columns - 1, receives[0], receives[1])[kind]
        return jnp.where((mask_ref[c, kind] == 1) & inside, 1.0, 0.0)

    def self_blocks(c, image, a_kind, b_kind):
        at = c * IMAGES + image
        gradients(strips[c, image], at)

        def form(k):
            x, y = group(grad_x, at, k), group(grad_y, at, k)
            return (x * x, x * y, y * y)

        base = c * (QROWS * LANES)
        for index, entry in enumerate(column_moments(Products(groups, form), width, True)):
            for moment, value in enumerate(entry):
                spot = index * QUAD + moment
                if a_kind is not None:
                    add(base + SUM_AT + spot, exists(c, a_kind) * value)
                if b_kind is not None:
                    put(base + SELF_AT[b_kind] + spot, value)

    def pair_blocks(kind, c, at_a, at_b, image_a, image_b):
        there = exists(c, kind)
        base = c * (QROWS * LANES)
        for p, ref in enumerate((grad_x, grad_y)):

            def cross(k):
                value = group(ref, at_a, k)
                return (value * group(grad_x, at_b, k), value * group(grad_y, at_b, k))

            for q, entry in enumerate(column_moments(Products(groups, cross), width, True)):
                for moment, value in enumerate(entry):
                    put(base + PAIR_AT[kind] + (2 * p + q) * QUAD + moment, -there * value)

        misfit = image_a.astype(jnp.float32) - image_b.astype(jnp.float32)

        def pulls(k):
            miss = misfit[k * SUB : (k + 1) * SUB]
            return (
                group(grad_x, at_a, k) * miss,
                group(grad_y, at_a, k) * miss,
                group(grad_x, at_b, k) * miss,
                group(grad_y, at_b, k) * miss,
            )

        for index, entry in enumerate(column_moments(Products(groups, pulls), width, False)):
            side, p = divmod(index, 2)
            for weight, value in zip((2, 0, 1), entry):
                if side:
                    put(base + PULL_B_AT + 6 * kind + 3 * p + weight, there * value)
                else:
                    add(base + PULL_A_AT + 3 * p + weight, -there * value)

    @pl.loop(0, columns)
    def _(c):
        self_blocks(c, 4, 2, 2)
        self_blocks(c, 3, 1, None)
        self_blocks(c, 2, None, 1)

    @pl.loop(0, columns - 1)
    def _(c):
        self_blocks(c, 1, 0, None)
        self_blocks(c + 1, 0, None, 0)
        pair_blocks(0, c, c * IMAGES + 1, (c + 1) * IMAGES, strips[c, 1], strips[c + 1, 0])

    ones = jnp.ones((SUB, LANES), jnp.bfloat16)
    lane = lax.broadcasted_iota(jnp.int32, (1, LANES), 1)
    contract = (((1,), (1,)), ((), ()))
    mine = pl.multiple_of(me * per_device, SUB)

    def line_of(c, h):
        part = rows[(c * QROWS + h) * LANES : (c * QROWS + h + 1) * LANES, :]
        high = part.astype(jnp.bfloat16)
        low = (part - high.astype(jnp.float32)).astype(jnp.bfloat16)
        summed = lax.dot_general(ones, high, contract, preferred_element_type=jnp.float32)
        summed = summed + lax.dot_general(ones, low, contract, preferred_element_type=jnp.float32)
        return summed[0:1] * (1.0 / (height * width))

    for c in range(columns):
        line = line_of(c, 0)
        for kind in range(KINDS):
            for axis, extent in ((0, width), (1, height)):
                shift = offset_ref[c, axis, kind].astype(jnp.float32) / extent
                line = jnp.where(lane == OFFSET_AT + 2 * kind + axis, shift, line)
            line = jnp.where(lane == EXISTS_AT + kind, exists(c, kind), line)
        line = jnp.where(lane == STIFF_AT, stiff_ref[c], line)
        early[pl.ds(mine + c, 1), :] = line

    def send_all(ref, stage):
        @pl.loop(1, count)
        def _(step):
            pltpu.make_async_remote_copy(
                src_ref=ref.at[pl.ds(mine, columns)],
                dst_ref=ref.at[pl.ds(mine, columns)],
                send_sem=gather_send.at[stage],
                recv_sem=gather_recv.at[stage],
                device_id=device(step),
                device_id_type=MESH,
            ).start()

    def wait_all(ref, sem):
        others = ref.at[pl.ds(0, (count - 1) * columns)]
        pltpu.make_async_copy(others, others, sem).wait()

    send_all(early, 0)

    for kind in (1, 0):

        @pl.when(receives[kind])
        def _():
            @pl.loop(0, columns)
            def _(c):
                strip_copy(kind, c).wait_recv()
                image = ENDS[kind + 1][0]
                at_b = own_images + kind * columns + c
                gradients(landed[kind, c], at_b)
                pair_blocks(
                    kind + 1, c, c * IMAGES + image, at_b, strips[c, image], landed[kind, c]
                )

    for c in range(columns):
        late[pl.ds(mine + c, 1), :] = line_of(c, 1)

    send_all(late, 1)

    tiles = columns * count
    padded = round_up(tiles, LANES)

    def receive(ref, h):
        wait_all(ref, gather_recv.at[h])
        parts = [ref[pl.ds(c, count, stride=per_device), :] for c in range(columns)]
        if padded > tiles:
            parts.append(jnp.zeros((padded - tiles, LANES), jnp.float32))
        table[h * LANES : (h + 1) * LANES, :] = jnp.concatenate(parts, axis=0).T

    receive(early, 0)

    sublane = lax.broadcasted_iota(jnp.int32, (SUB, padded), 0)
    place = lax.broadcasted_iota(jnp.int32, (SUB, padded), 1)
    picks = [sublane == i for i in range(6)]

    def entry(at):
        return table[at : at + 1, :]

    def stacked(spots):
        total = jnp.zeros((SUB, padded), jnp.float32)
        for pick, at in zip(picks, spots):
            total = jnp.where(pick, entry(at), total)
        return total

    def block_at(base, field):
        return [
            stacked(
                [base + field[p][q] * QUAD + MOMENT[a][b] for p in range(2) for a in range(3)]
            )
            for q in range(2)
            for b in range(3)
        ]

    own_field = ((0, 1), (1, 2))
    pair_field = ((0, 1), (2, 3))

    def to_next(array, by):
        return pltpu.roll(array, by, 1)

    def from_next(array, by):
        return pltpu.roll(array, padded - by, 1)

    def shift_rows(vector, offset):
        return vector + offset * jnp.where(sublane < 3, vector[2:3], vector[5:6])

    def shift_columns(block, offset):
        du, dv = offset[0:1], offset[1:2]
        out = []
        for p in range(2):
            last = block[3 * p + 2]
            out += [block[3 * p] + du * last, block[3 * p + 1] + dv * last, last]
        return out

    shifts = (count, 1, tile_rows)
    stiffness = jnp.where(place < tiles, entry(STIFF_AT), 1.0)
    diagonal = [
        column + jnp.where(pick, stiffness, 0.0)
        for pick, column in zip(picks, block_at(SUM_AT, own_field))
    ]
    offsets = []
    for kind in range(KINDS):
        by = shifts[kind]
        du, dv = entry(OFFSET_AT + 2 * kind), entry(OFFSET_AT + 2 * kind + 1)
        offset = jnp.where(picks[0] | picks[3], du, jnp.where(picks[1] | picks[4], dv, 0.0))
        offsets.append(offset)
        offset_b = to_next(offset, by)
        there_b = to_next(jnp.broadcast_to(entry(EXISTS_AT + kind), offset.shape), by)
        block_b = shift_columns(block_at(SELF_AT[kind], own_field), offset_b)
        for j in range(6):
            diagonal[j] = diagonal[j] + there_b * shift_rows(block_b[j], offset_b)

    inverse = inverse_columns(diagonal, sublane)

    receive(late, 1)
    load = stacked([PULL_A_AT + i for i in range(6)])
    couplings = []
    for kind in range(KINDS):
        by, offset = shifts[kind], offsets[kind]
        pull_b = stacked([PULL_B_AT + 6 * kind + i for i in range(6)])
        load = load + to_next(shift_rows(pull_b, offset), by)
        coupling = shift_columns(block_at(PAIR_AT[kind], pair_field), offset)
        couplings.append((coupling, transposed_columns(coupling, sublane), by))

    def multiply(vector):
        result = apply_columns(diagonal, vector)
        for coupling, flipped, by in couplings:
            result = result + apply_columns(coupling, from_next(vector, by))
            result = result + to_next(apply_columns(flipped, vector), by)
        return result

    def total(array):
        return jnp.sum(jnp.sum(array, axis=0, keepdims=True), axis=1, keepdims=True)

    residual = load
    scaled = apply_columns(inverse, residual)
    product = multiply(scaled)
    rho_now, curve = total(residual * scaled), total(scaled * product)
    step_size = rho_now / curve
    direction, carried = scaled, product
    update = jnp.zeros_like(load)
    for step in range(ITERS):
        update = update + step_size * direction
        residual = residual - step_size * carried
        if step + 1 < ITERS:
            scaled = apply_columns(inverse, residual)
            product = multiply(scaled)
            rho_next, curve = total(residual * scaled), total(scaled * product)
            ratio = rho_next / rho_now
            step_size = rho_next / (curve - ratio * rho_next / step_size)
            direction = scaled + ratio * direction
            carried = product + ratio * carried
            rho_now = rho_next

    turn = sublane[:, :LANES] == place[:, :LANES]
    for index, values in enumerate((update, residual)):
        for c in range(columns):
            own = jnp.sum(jnp.where(place == c * count + me, values, 0.0), axis=1, keepdims=True)
            line = jnp.sum(jnp.where(turn, own, 0.0), axis=0, keepdims=True)
            out_ref[index, c : c + 1, :] = line[:, 0:6]

    wait_all(early, gather_send.at[0])
    wait_all(late, gather_send.at[1])
    for kind in range(2):

        @pl.when(sends[kind])
        def _():
            for c in range(columns):
                strip_copy(kind, c).wait_send()


def shards(tile_strips, pair_mask, strip_offset, stiffness):
    _, _, columns, images, height, width = tile_strips.shape
    sections = lax.axis_size("sec")
    tile_rows = lax.axis_size("tile")
    count = sections * tile_rows
    per_device = round_up(columns, SUB)
    held = columns * (IMAGES + 2) * height
    padded = round_up(columns * count, LANES)
    both = pl.pallas_call(
        functools.partial(kernel, sections, tile_rows),
        out_shape=jax.ShapeDtypeStruct((2, columns, 6), jnp.float32),
        in_specs=[pl.BlockSpec(memory_space=pltpu.HBM)] * 4,
        out_specs=pl.BlockSpec(memory_space=pltpu.VMEM),
        scratch_shapes=[
            pltpu.VMEM((columns, images, height, width), jnp.bfloat16),
            pltpu.VMEM((2, columns, height, width), jnp.bfloat16),
            pltpu.VMEM((held, width), jnp.float32),
            pltpu.VMEM((held, width), jnp.float32),
            pltpu.VMEM((columns * QROWS * LANES, LANES), jnp.float32),
            pltpu.VMEM((count * per_device, LANES), jnp.float32),
            pltpu.VMEM((count * per_device, LANES), jnp.float32),
            pltpu.VMEM((QROWS * LANES, padded), jnp.float32),
            pltpu.SMEM((columns, KINDS), jnp.int32),
            pltpu.SMEM((columns, 2, KINDS), jnp.int32),
            pltpu.SMEM((columns,), jnp.float32),
            pltpu.SemaphoreType.DMA((4,)),
            pltpu.SemaphoreType.DMA((2, columns)),
            pltpu.SemaphoreType.DMA((2, columns)),
            pltpu.SemaphoreType.DMA((2,)),
            pltpu.SemaphoreType.DMA((2,)),
        ],
        compiler_params=pltpu.CompilerParams(
            collective_id=0, has_side_effects=True, vmem_limit_bytes=54784 * 1024
        ),
    )(
        tile_strips[0, 0],
        pair_mask[0, 0],
        jnp.swapaxes(strip_offset[0, 0], 1, 2),
        stiffness[0, 0],
    )
    both = jnp.swapaxes(both, 1, 2).reshape(2, 6, 1, 1, columns)
    return both[0], both[1]


def solution(mesh):
    return jax.shard_map(
        shards,
        mesh=mesh,
        in_specs=(
            P("sec", "tile", None, None, None, None),
            P("sec", "tile", None, None),
            P("sec", "tile", None, None, None),
            P("sec", "tile", None),
        ),
        out_specs=(P(None, "sec", "tile", None), P(None, "sec", "tile", None)),
        check_vma=False,
    )
```

```python
import functools

import jax
import jax.numpy as jnp
from jax import lax
from jax.experimental import pallas as pl
from jax.experimental.pallas import tpu as pltpu
from jax.sharding import PartitionSpec as P

ITERS = 3
LANES = 128
SUB = 8
IMAGES = 5
KINDS = 3
QROWS = 2
MESH = pl.DeviceIdType.MESH

QUAD = 6
MOMENT = ((3, 4, 1), (4, 5, 2), (1, 2, 0))
SELF = 3 * QUAD
CROSS = 4 * QUAD
SUM_AT = 0
SELF_AT = (SELF, 2 * SELF, 3 * SELF)
OFFSET_AT = 96
EXISTS_AT = 102
STIFF_AT = 105
PAIR_AT = (LANES, LANES + CROSS, LANES + 2 * CROSS)
PULL_A_AT = LANES + 3 * CROSS
PULL_B_AT = PULL_A_AT + 6
ENDS = ((1, 0), (3, 2), (4, 4))


def round_up(value, unit):
    return (value + unit - 1) // unit * unit


def column_moments(fields, width, quadratic):
    groups = fields.groups
    sums = None
    for k in range(groups):
        values = fields(k)
        if sums is None:
            sums = [[value] * (3 if quadratic else 2) for value in values]
        else:
            for entry, value in zip(sums, values):
                entry[0] = entry[0] + value
                entry[1] = entry[1] + entry[0]
                if quadratic:
                    entry[2] = entry[2] + entry[1]
    height = groups * SUB
    step = SUB / height
    row = lax.broadcasted_iota(jnp.int32, (SUB, LANES), 0).astype(jnp.float32)
    column = lax.broadcasted_iota(jnp.int32, (SUB, width), 1).astype(jnp.float32)
    edge = row / height + 0.5
    u = column / width - 0.5

    def fold(array):
        total = array[:, :LANES]
        for start in range(LANES, width, LANES):
            total = total + array[:, start : start + LANES]
        return total

    out = []
    for entry in sums:
        first, second = fold(entry[0]), fold(entry[1])
        scaled = u * entry[0]
        along = fold(scaled)
        moments = [first, along, edge * first - step * second]
        if quadratic:
            third = 2.0 * fold(entry[2]) - second
            moments += [
                fold(u * scaled),
                edge * along - step * fold(u * entry[1]),
                edge * (edge * first - (2.0 * step) * second) + (step * step) * third,
            ]
        out.append([jnp.sum(moment, axis=0, keepdims=True) for moment in moments])
    return out


class Products:
    def __init__(self, groups, form):
        self.groups = groups
        self.form = form

    def __call__(self, k):
        return self.form(k)


def apply_columns(columns, vector):
    total = columns[0] * vector[0:1]
    for j in range(1, 6):
        total = total + columns[j] * vector[j : j + 1]
    return total


def inverse_columns(columns, sublane):
    columns = list(columns)
    for p in range(6):
        pivot = 1.0 / columns[p][p : p + 1]
        here = sublane == p
        lead = columns[p]
        for j in range(6):
            if j != p:
                ratio = columns[j][p : p + 1] * pivot
                columns[j] = jnp.where(here, ratio, columns[j] - lead * ratio)
        columns[p] = jnp.where(here, pivot, -lead * pivot)
    return columns


def transposed_columns(columns, sublane):
    out = []
    for i in range(6):
        total = jnp.zeros_like(columns[0])
        for j in range(6):
            total = jnp.where(sublane == j, columns[j][i : i + 1], total)
        out.append(total)
    return out


def kernel(
    sections,
    tile_rows,
    strips_hbm,
    mask_hbm,
    offset_hbm,
    stiff_hbm,
    out_ref,
    strips,
    landed,
    grad_x,
    grad_y,
    rows,
    early,
    late,
    table,
    mask_ref,
    offset_ref,
    stiff_ref,
    local_sem,
    strip_send,
    strip_recv,
    gather_send,
    gather_recv,
    all_in,
):
    columns, _, height, width = strips.shape
    count = sections * tile_rows
    per_device = early.shape[0] // count
    groups = height // SUB
    own_images = columns * IMAGES
    section = lax.axis_index("sec")
    tile_row = lax.axis_index("tile")
    me = section * tile_rows + tile_row

    def device(step):
        other = lax.rem(me + step, count)
        return (other // tile_rows, lax.rem(other, tile_rows))

    def along_tile(step):
        return (section, lax.rem(tile_row + step, tile_rows))

    def along_sec(step):
        return (lax.rem(section + step, sections), tile_row)

    barrier = pltpu.get_barrier_semaphore()

    def greet(semaphore, size, target):
        @pl.loop(1, size)
        def _(step):
            pl.semaphore_signal(semaphore, inc=1, device_id=target(step), device_id_type=MESH)

    greet(barrier, sections, along_sec)
    greet(barrier, tile_rows, along_tile)

    local = [
        pltpu.make_async_copy(source, target, local_sem.at[index])
        for index, (source, target) in enumerate(
            (
                (strips_hbm, strips),
                (mask_hbm, mask_ref),
                (offset_hbm, offset_ref),
                (stiff_hbm, stiff_ref),
            )
        )
    ]
    for copy in local:
        copy.start()

    first = lax.broadcasted_iota(jnp.int32, (height, height), 0)
    second = lax.broadcasted_iota(jnp.int32, (height, height), 1)
    gap = second - first
    down = jnp.where(gap == 1, 0.5, jnp.where(gap == -1, -0.5, 0.0)).astype(jnp.bfloat16)
    rows[...] = jnp.zeros_like(rows)

    pl.semaphore_wait(barrier, tile_rows + sections - 2)

    def strip_copy(kind, c):
        target = (section, tile_row - 1) if kind == 0 else (section - 1, tile_row)
        return pltpu.make_async_remote_copy(
            src_ref=strips_hbm.at[c, 2 if kind == 0 else 4],
            dst_ref=landed.at[kind, c],
            send_sem=strip_send.at[kind, c],
            recv_sem=strip_recv.at[kind, c],
            device_id=target,
            device_id_type=MESH,
        )

    sends = (tile_row > 0, section > 0)
    receives = (tile_row < tile_rows - 1, section < sections - 1)
    for kind in range(2):

        @pl.when(sends[kind])
        def _():
            for c in range(columns):
                strip_copy(kind, c).start()

    greet(all_in, tile_rows, along_tile)

    for copy in local:
        copy.wait()

    column = lax.broadcasted_iota(jnp.int32, (height, width), 1)

    def gradients(image, at):
        values = image.astype(jnp.float32)
        before = jnp.where(column == 0, 0.0, pltpu.roll(values, 1, 1))
        after = jnp.where(column == width - 1, 0.0, pltpu.roll(values, width - 1, 1))
        spot = pl.ds(pl.multiple_of(at * height, SUB), height)
        grad_x[spot, :] = (after - before) * 0.5
        grad_y[spot, :] = jnp.dot(down, image, preferred_element_type=jnp.float32)

    def group(ref, image, k):
        return ref[pl.ds(pl.multiple_of(image * height + k * SUB, SUB), SUB), :]

    def put(row, value):
        rows[pl.ds(row, 1), :] = value

    def add(row, value):
        rows[pl.ds(row, 1), :] = rows[pl.ds(row, 1), :] + value

    def exists(c, kind):
        inside = (jnp.int32(c) < columns - 1, receives[0], receives[1])[kind]
        return jnp.where((mask_ref[c, kind] == 1) & inside, 1.0, 0.0)

    def self_blocks(c, image, a_kind, b_kind):
        at = c * IMAGES + image
        gradients(strips[c, image], at)

        def form(k):
            x, y = group(grad_x, at, k), group(grad_y, at, k)
            return (x * x, x * y, y * y)

        base = c * (QROWS * LANES)
        for index, entry in enumerate(column_moments(Products(groups, form), width, True)):
            for moment, value in enumerate(entry):
                spot = index * QUAD + moment
                if a_kind is not None:
                    add(base + SUM_AT + spot, exists(c, a_kind) * value)
                if b_kind is not None:
                    put(base + SELF_AT[b_kind] + spot, value)

    def pair_blocks(kind, c, at_a, at_b, image_a, image_b):
        there = exists(c, kind)
        base = c * (QROWS * LANES)
        for p, ref in enumerate((grad_x, grad_y)):

            def cross(k):
                value = group(ref, at_a, k)
                return (value * group(grad_x, at_b, k), value * group(grad_y, at_b, k))

            for q, entry in enumerate(column_moments(Products(groups, cross), width, True)):
                for moment, value in enumerate(entry):
                    put(base + PAIR_AT[kind] + (2 * p + q) * QUAD + moment, -there * value)

        misfit = image_a.astype(jnp.float32) - image_b.astype(jnp.float32)

        def pulls(k):
            miss = misfit[k * SUB : (k + 1) * SUB]
            return (
                group(grad_x, at_a, k) * miss,
                group(grad_y, at_a, k) * miss,
                group(grad_x, at_b, k) * miss,
                group(grad_y, at_b, k) * miss,
            )

        for index, entry in enumerate(column_moments(Products(groups, pulls), width, False)):
            side, p = divmod(index, 2)
            for weight, value in zip((2, 0, 1), entry):
                if side:
                    put(base + PULL_B_AT + 6 * kind + 3 * p + weight, there * value)
                else:
                    add(base + PULL_A_AT + 3 * p + weight, -there * value)

    @pl.loop(0, columns)
    def _(c):
        self_blocks(c, 4, 2, 2)
        self_blocks(c, 3, 1, None)
        self_blocks(c, 2, None, 1)

    @pl.loop(0, columns - 1)
    def _(c):
        self_blocks(c, 1, 0, None)
        self_blocks(c + 1, 0, None, 0)
        pair_blocks(0, c, c * IMAGES + 1, (c + 1) * IMAGES, strips[c, 1], strips[c + 1, 0])

    ones = jnp.ones((SUB, LANES), jnp.bfloat16)
    lane = lax.broadcasted_iota(jnp.int32, (1, LANES), 1)
    contract = (((1,), (1,)), ((), ()))
    mine = pl.multiple_of(me * per_device, SUB)

    def line_of(c, h):
        part = rows[(c * QROWS + h) * LANES : (c * QROWS + h + 1) * LANES, :]
        high = part.astype(jnp.bfloat16)
        low = (part - high.astype(jnp.float32)).astype(jnp.bfloat16)
        summed = lax.dot_general(ones, high, contract, preferred_element_type=jnp.float32)
        summed = summed + lax.dot_general(ones, low, contract, preferred_element_type=jnp.float32)
        return summed[0:1] * (1.0 / (height * width))

    for c in range(columns):
        line = line_of(c, 0)
        for kind in range(KINDS):
            for axis, extent in ((0, width), (1, height)):
                shift = offset_ref[c, axis, kind].astype(jnp.float32) / extent
                line = jnp.where(lane == OFFSET_AT + 2 * kind + axis, shift, line)
            line = jnp.where(lane == EXISTS_AT + kind, exists(c, kind), line)
        line = jnp.where(lane == STIFF_AT, stiff_ref[c], line)
        early[pl.ds(mine + c, 1), :] = line

    def send_all(ref, stage):
        @pl.loop(1, count)
        def _(step):
            pltpu.make_async_remote_copy(
                src_ref=ref.at[pl.ds(mine, columns)],
                dst_ref=ref.at[pl.ds(mine, columns)],
                send_sem=gather_send.at[stage],
                recv_sem=gather_recv.at[stage],
                device_id=device(step),
                device_id_type=MESH,
            ).start()

    def wait_all(ref, sem):
        others = ref.at[pl.ds(0, (count - 1) * columns)]
        pltpu.make_async_copy(others, others, sem).wait()

    pl.semaphore_wait(all_in, tile_rows - 1)
    send_all(early, 0)

    for kind in (1, 0):

        @pl.when(receives[kind])
        def _():
            @pl.loop(0, columns)
            def _(c):
                strip_copy(kind, c).wait_recv()
                image = ENDS[kind + 1][0]
                at_b = own_images + kind * columns + c
                gradients(landed[kind, c], at_b)
                pair_blocks(
                    kind + 1, c, c * IMAGES + image, at_b, strips[c, image], landed[kind, c]
                )

    for c in range(columns):
        late[pl.ds(mine + c, 1), :] = line_of(c, 1)

    send_all(late, 1)

    tiles = columns * count
    padded = round_up(tiles, LANES)

    def receive(ref, h):
        wait_all(ref, gather_recv.at[h])
        parts = [ref[pl.ds(c, count, stride=per_device), :] for c in range(columns)]
        if padded > tiles:
            parts.append(jnp.zeros((padded - tiles, LANES), jnp.float32))
        table[h * LANES : (h + 1) * LANES, :] = jnp.concatenate(parts, axis=0).T

    receive(early, 0)

    sublane = lax.broadcasted_iota(jnp.int32, (SUB, padded), 0)
    place = lax.broadcasted_iota(jnp.int32, (SUB, padded), 1)
    picks = [sublane == i for i in range(6)]

    def entry(at):
        return table[at : at + 1, :]

    def stacked(spots):
        total = jnp.zeros((SUB, padded), jnp.float32)
        for pick, at in zip(picks, spots):
            total = jnp.where(pick, entry(at), total)
        return total

    def block_at(base, field):
        return [
            stacked(
                [base + field[p][q] * QUAD + MOMENT[a][b] for p in range(2) for a in range(3)]
            )
            for q in range(2)
            for b in range(3)
        ]

    own_field = ((0, 1), (1, 2))
    pair_field = ((0, 1), (2, 3))

    def to_next(array, by):
        return pltpu.roll(array, by, 1)

    def from_next(array, by):
        return pltpu.roll(array, padded - by, 1)

    def shift_rows(vector, offset):
        return vector + offset * jnp.where(sublane < 3, vector[2:3], vector[5:6])

    def shift_columns(block, offset):
        du, dv = offset[0:1], offset[1:2]
        out = []
        for p in range(2):
            last = block[3 * p + 2]
            out += [block[3 * p] + du * last, block[3 * p + 1] + dv * last, last]
        return out

    shifts = (count, 1, tile_rows)
    stiffness = jnp.where(place < tiles, entry(STIFF_AT), 1.0)
    diagonal = [
        column + jnp.where(pick, stiffness, 0.0)
        for pick, column in zip(picks, block_at(SUM_AT, own_field))
    ]
    offsets = []
    for kind in range(KINDS):
        by = shifts[kind]
        du, dv = entry(OFFSET_AT + 2 * kind), entry(OFFSET_AT + 2 * kind + 1)
        offset = jnp.where(picks[0] | picks[3], du, jnp.where(picks[1] | picks[4], dv, 0.0))
        offsets.append(offset)
        offset_b = to_next(offset, by)
        there_b = to_next(jnp.broadcast_to(entry(EXISTS_AT + kind), offset.shape), by)
        block_b = shift_columns(block_at(SELF_AT[kind], own_field), offset_b)
        for j in range(6):
            diagonal[j] = diagonal[j] + there_b * shift_rows(block_b[j], offset_b)

    inverse = inverse_columns(diagonal, sublane)

    receive(late, 1)
    load = stacked([PULL_A_AT + i for i in range(6)])
    couplings = []
    for kind in range(KINDS):
        by, offset = shifts[kind], offsets[kind]
        pull_b = stacked([PULL_B_AT + 6 * kind + i for i in range(6)])
        load = load + to_next(shift_rows(pull_b, offset), by)
        coupling = shift_columns(block_at(PAIR_AT[kind], pair_field), offset)
        couplings.append((coupling, transposed_columns(coupling, sublane), by))

    def multiply(vector):
        result = apply_columns(diagonal, vector)
        for coupling, flipped, by in couplings:
            result = result + apply_columns(coupling, from_next(vector, by))
            result = result + to_next(apply_columns(flipped, vector), by)
        return result

    def total(array):
        return jnp.sum(jnp.sum(array, axis=0, keepdims=True), axis=1, keepdims=True)

    residual = load
    scaled = apply_columns(inverse, residual)
    product = multiply(scaled)
    rho_now, curve = total(residual * scaled), total(scaled * product)
    step_size = rho_now / curve
    direction, carried = scaled, product
    update = jnp.zeros_like(load)
    for step in range(ITERS):
        update = update + step_size * direction
        residual = residual - step_size * carried
        if step + 1 < ITERS:
            scaled = apply_columns(inverse, residual)
            product = multiply(scaled)
            rho_next, curve = total(residual * scaled), total(scaled * product)
            ratio = rho_next / rho_now
            step_size = rho_next / (curve - ratio * rho_next / step_size)
            direction = scaled + ratio * direction
            carried = product + ratio * carried
            rho_now = rho_next

    turn = sublane[:, :LANES] == place[:, :LANES]
    for index, values in enumerate((update, residual)):
        for c in range(columns):
            own = jnp.sum(jnp.where(place == c * count + me, values, 0.0), axis=1, keepdims=True)
            line = jnp.sum(jnp.where(turn, own, 0.0), axis=0, keepdims=True)
            out_ref[index, c : c + 1, :] = line[:, 0:6]

    wait_all(early, gather_send.at[0])
    wait_all(late, gather_send.at[1])
    for kind in range(2):

        @pl.when(sends[kind])
        def _():
            for c in range(columns):
                strip_copy(kind, c).wait_send()


def shards(tile_strips, pair_mask, strip_offset, stiffness):
    _, _, columns, images, height, width = tile_strips.shape
    sections = lax.axis_size("sec")
    tile_rows = lax.axis_size("tile")
    count = sections * tile_rows
    per_device = round_up(columns, SUB)
    held = columns * (IMAGES + 2) * height
    padded = round_up(columns * count, LANES)
    both = pl.pallas_call(
        functools.partial(kernel, sections, tile_rows),
        out_shape=jax.ShapeDtypeStruct((2, columns, 6), jnp.float32),
        in_specs=[pl.BlockSpec(memory_space=pltpu.HBM)] * 4,
        out_specs=pl.BlockSpec(memory_space=pltpu.VMEM),
        scratch_shapes=[
            pltpu.VMEM((columns, images, height, width), jnp.bfloat16),
            pltpu.VMEM((2, columns, height, width), jnp.bfloat16),
            pltpu.VMEM((held, width), jnp.float32),
            pltpu.VMEM((held, width), jnp.float32),
            pltpu.VMEM((columns * QROWS * LANES, LANES), jnp.float32),
            pltpu.VMEM((count * per_device, LANES), jnp.float32),
            pltpu.VMEM((count * per_device, LANES), jnp.float32),
            pltpu.VMEM((QROWS * LANES, padded), jnp.float32),
            pltpu.SMEM((columns, KINDS), jnp.int32),
            pltpu.SMEM((columns, 2, KINDS), jnp.int32),
            pltpu.SMEM((columns,), jnp.float32),
            pltpu.SemaphoreType.DMA((4,)),
            pltpu.SemaphoreType.DMA((2, columns)),
            pltpu.SemaphoreType.DMA((2, columns)),
            pltpu.SemaphoreType.DMA((2,)),
            pltpu.SemaphoreType.DMA((2,)),
            pltpu.SemaphoreType.REGULAR,
        ],
        compiler_params=pltpu.CompilerParams(
            collective_id=0, has_side_effects=True, vmem_limit_bytes=54784 * 1024
        ),
    )(
        tile_strips[0, 0],
        pair_mask[0, 0],
        jnp.swapaxes(strip_offset[0, 0], 1, 2),
        stiffness[0, 0],
    )
    both = jnp.swapaxes(both, 1, 2).reshape(2, 6, 1, 1, columns)
    return both[0], both[1]


def solution(mesh):
    return jax.shard_map(
        shards,
        mesh=mesh,
        in_specs=(
            P("sec", "tile", None, None, None, None),
            P("sec", "tile", None, None),
            P("sec", "tile", None, None, None),
            P("sec", "tile", None),
        ),
        out_specs=(P(None, "sec", "tile", None), P(None, "sec", "tile", None)),
        check_vma=False,
    )
```
